32 devices in a mesh: expert: 8 (over z, x), tensor: 4 (over y, core).
Axes of the slice: x: 2, y: 2, z: 4, core: 2. Of those that a mesh axis runs over, the one named last changes fastest.
Arguments:
- tokens: bfloat16 [2, 1024, 2048], P(None, 'expert'), may hold values from -6 to 6
- out_grad: bfloat16 [2, 1024, 2048], P(None, 'expert'), may hold values from -6 to 6
- routes: int32 [2, 1024, 8], P(None, 'expert'), may hold values from 0 to 31, all different within a row; in each aligned block of 128 rows (0 to 127, 128 to 255, ..., all dimensions but the last counted through in order) at most 64 rows name the same one
- norm1_gain: float32 [2048], replicated, may hold values from 0.1 to 1.9
- w_query: bfloat16 [2048, 2048], P(None, 'tensor'), may hold values from -0.125 to 0.125
- w_key: bfloat16 [2048, 2048], P(None, 'tensor'), may hold values from -0.125 to 0.125
- w_value: bfloat16 [2048, 2048], P(None, 'tensor'), may hold values from -0.125 to 0.125
- query_gain: float32 [16, 128], P('tensor'), may hold values from 1 to 2
- key_gain: float32 [16, 128], P('tensor'), may hold values from 1 to 2
- w_output: bfloat16 [2048, 2048], P('tensor'), may hold values from -1 to 1
- norm2_gain: float32 [2048], replicated, may hold values from 0.1 to 1.9
- w_router: bfloat16 [2048, 32], replicated, may hold values from -0.0625 to 0.0625
- w_gate: bfloat16 [32, 2048, 1024], P('expert', None, 'tensor'), may hold values from -0.125 to 0.125
- w_up: bfloat16 [32, 2048, 1024], P('expert', None, 'tensor'), may hold values from -0.125 to 0.125
- w_down: bfloat16 [32, 1024, 2048], P('expert', 'tensor'), may hold values from -6 to 6
Outputs:
- layer_out: bfloat16 [2, 1024, 2048], P(None, 'expert', 'tensor')
- tokens_grad: float32 [2, 1024, 2048], P(None, 'expert')
- norm1_gain_grad: float32 [2048], P('expert')
- w_query_grad: float32 [2048, 2048], P('expert', 'tensor')
- w_key_grad: float32 [2048, 2048], P('expert', 'tensor')
- w_value_grad: float32 [2048, 2048], P('expert', 'tensor')
- query_gain_grad: float32 [16, 128], P('tensor', 'expert')
- key_gain_grad: float32 [16, 128], P('tensor', 'expert')
- w_output_grad: float32 [2048, 2048], P('tensor', 'expert')
- norm2_gain_grad: float32 [2048], P('expert')
- w_router_grad: float32 [2048, 32], P('expert')
- w_gate_grad: float32 [32, 2048, 1024], P('expert', None, 'tensor')
- w_up_grad: float32 [32, 2048, 1024], P('expert', None, 'tensor')
- w_down_grad: float32 [32, 1024, 2048], P('expert', 'tensor')
The draws below stay inside these ranges and needn't reach their ends.
Inputs may be any that keep to these rules, and one draw needn't show every extreme that they name: `routes`: A token's 8 experts differ. In each micro-batch, the 128 tokens of one device name any expert at most 64 times, a bound that some block reaches in some of these blocks.
All inputs are finite; a program needn't handle non-finite values.
Results may differ from the reference program's by a relative error of at most 0.03.
Values may be sent and summed in bfloat16 or wider, within the bound.
No kernel may reach another device: no remote copies, remote signals or barrier semaphores. Data moves between devices by JAX's collectives and lax.ppermute only.
A program may use at most 256 MiB of HBM per device.

```python
import math
import jax
import jax.numpy as jnp
import numpy as np
from jax import lax

D = 2048
HEADS = 16
HEAD_DIM = 128
FF = 1024
TOPK = 8
TOK_DEV = 128
MB = 2
EXPERTS = 32
SEQ = 1024
CAP = 64
N_EXPERT = 8
N_TENSOR = 4


def steps_of(key, shape, cuts, least, top_value):
    loudness, own = 1.0, jax.random.fold_in(key, 6)
    for axis_at, parts in cuts:
        steps = jnp.exp(jax.random.uniform(jax.random.fold_in(own, axis_at), (parts,), jnp.float32, least / len(cuts), top_value / len(cuts)))
        loudness = loudness * jnp.repeat(steps, shape[axis_at] // parts).reshape([-1 if axis == axis_at else 1 for axis in range(len(shape))])
    return loudness


def deal_out(own_key, own, number, rows, number_of, top, bound, skew):
    order = jax.random.permutation(own_key, number_of)
    crowded, ordinary = shares(number_of, rows * top, bound, skew, True), shares(number_of, rows * top, bound, skew, False)
    places = jnp.arange(number_of)

    def named(lengths, rotation):
        used = int((lengths > 0).sum())
        fixed = max(1, used // 4)
        moved = fixed + (places - fixed + rotation * (used - fixed)) % max(1, number_of - fixed)
        return jnp.zeros((number_of,), jnp.int32).at[order[jnp.where(places < fixed, places, moved)]].set(jnp.asarray(lengths, jnp.int32))

    lengths = jnp.where(number % 4 == 0, named(crowded, number // 4), named(ordinary, number - number // 4 - 1))
    mixed = jax.random.permutation(jax.random.fold_in(own, 3), number_of)
    giver, sink = mixed[0:number_of // 2 * 2:2], mixed[1:number_of // 2 * 2:2]
    slack = jnp.minimum(lengths[giver] - 1, bound - lengths[sink]) // 2
    slack = jnp.where((giver == order[0]) | (sink == order[0]) | (lengths[sink] == 0), 0, jnp.maximum(slack, 0))
    moved = jax.random.randint(jax.random.fold_in(own, 4), (number_of // 2,), 0, 1 << 20) % (slack + 1)
    lengths = lengths.at[giver].add(-moved).at[sink].add(moved)
    members = jnp.searchsorted(jnp.cumsum(lengths), jnp.arange(rows * top), side="right").astype(jnp.int32)
    grid = members.reshape(top, rows).T
    grid = grid[jax.random.permutation(jax.random.fold_in(own, 1), rows)]
    rotation = jax.random.randint(jax.random.fold_in(own, 2), (rows, 1), 0, top)
    return jnp.take_along_axis(grid, (jnp.arange(top)[None, :] + rotation) % top, axis=1)


def shares(count, total, most, skew, full):
    weights = [(1 << 20) // math.isqrt(rank ** skew) + 1 for rank in range(1, count + 1)]
    largest = most if full else min(most, max(-(-total // count), total * weights[0] // sum(weights)))
    least = 1 if total - largest >= count - 1 else 0
    given, surplus = [largest] + [least] * (count - 1), total - largest - least * (count - 1)
    while surplus > 0:
        movable = [i for i in range(1, count) if given[i] < largest] or [i for i in range(1, count) if given[i] < most]
        mass, left = sum([weights[i] for i in movable]), surplus
        for i in movable:
            addition = min(most - given[i], max(1, left * weights[i] // mass), surplus)
            given[i] = given[i] + addition
            surplus = surplus - addition
    return np.array(given)


def bell_draw(stream_key, dims, scale, bound, cuts=(), kind=jnp.bfloat16):
    entries = jax.random.normal(stream_key, dims, jnp.float32) * scale
    if len(cuts) > 0:
        entries = steps_of(stream_key, dims, cuts, -0.22, 0.18) * entries
    return jnp.clip(entries, min=-bound, max=bound).astype(kind)


def setup_inputs(seed: int = 0) -> dict:
    streams_of = jax.random.split(jax.random.key(seed), 16)
    tokens = bell_draw(streams_of[0], (MB, SEQ, D), 1.0, 6.0, ((1, 8),))
    out_grad = bell_draw(streams_of[1], (MB, SEQ, D), 1.0, 6.0, ((1, 8),))
    routes_keys = jax.random.split(jax.random.fold_in(streams_of[2], 1), MB * SEQ // TOK_DEV)
    routes_turns = jax.random.permutation(jax.random.fold_in(streams_of[2], 3), MB * SEQ // TOK_DEV)
    routes = jax.vmap(lambda own, number: deal_out(jax.random.fold_in(streams_of[2], 2), own, number, TOK_DEV, EXPERTS, TOPK, CAP, 2))(routes_keys, routes_turns).reshape((MB, SEQ, TOPK))
    norm1_gain = jnp.clip(1.0 + 0.18 * jax.random.normal(streams_of[3], (D,), jnp.float32), 0.1, 1.9)
    w_query = bell_draw(streams_of[4], (D, D), D ** -0.5, 0.125, ((1, 4),))
    w_key = bell_draw(streams_of[5], (D, D), D ** -0.5, 0.125, ((1, 4),))
    w_value = bell_draw(streams_of[6], (D, D), D ** -0.5, 0.125, ((1, 4),))
    query_gain = jnp.clip(jnp.exp(math.log(2.0) - 0.6931472 * jax.random.uniform(streams_of[7], (HEADS, HEAD_DIM), jnp.float32) ** steps_of(streams_of[7], (HEADS, HEAD_DIM), ((0, 4),), -0.2, 0.2)), 1.0, 2.0)
    key_gain = jnp.clip(jnp.exp(math.log(2.0) - 0.6931472 * jax.random.uniform(streams_of[8], (HEADS, HEAD_DIM), jnp.float32) ** steps_of(streams_of[8], (HEADS, HEAD_DIM), ((0, 4),), -0.2, 0.2)), 1.0, 2.0)
    w_output = bell_draw(streams_of[9], (D, D), (D // 64) ** -0.5, 1.0, ((0, 4),))
    norm2_gain = jnp.clip(1.0 + 0.18 * jax.random.normal(streams_of[10], (D,), jnp.float32), 0.1, 1.9)
    w_router = bell_draw(streams_of[11], (D, EXPERTS), (4 * D) ** -0.5, 0.0625)
    w_gate = bell_draw(streams_of[12], (EXPERTS, D, FF), D ** -0.5, 0.125, ((0, 8), (2, 4)))
    w_up = bell_draw(streams_of[13], (EXPERTS, D, FF), D ** -0.5, 0.125, ((0, 8), (2, 4)))
    w_down = bell_draw(streams_of[14], (EXPERTS, FF, D), 1 ** -0.5, 6.0, ((0, 8), (1, 4)))
    return dict(tokens=tokens, out_grad=out_grad, routes=routes, norm1_gain=norm1_gain, w_query=w_query, w_key=w_key, w_value=w_value, query_gain=query_gain, key_gain=key_gain, w_output=w_output, norm2_gain=norm2_gain, w_router=w_router, w_gate=w_gate, w_up=w_up, w_down=w_down)


@jax.custom_vjp
def low(v):
    return lax.optimization_barrier(v.astype(jnp.bfloat16)).astype(jnp.float32)

@jax.custom_vjp
def low_back(v):
    return v

def low_keep(v):
    return (low(v), None)

def low_pass(kept, grad):
    return (grad,)

def back_keep(v):
    return (v, None)

def back_low(kept, grad):
    return (low(grad),)
low.defvjp(low_keep, low_pass)
low_back.defvjp(back_keep, back_low)
eps = 1e-05
theta_base = 10000.0
masked_score = -1e+30
highest = lax.Precision.HIGHEST

def rms_scale(operand):
    return lax.rsqrt(lax.optimization_barrier(jnp.mean(operand * operand, axis=-1, keepdims=True)) + eps)

def turn_half(operand):
    middle = operand.shape[-1] // 2
    return jnp.concatenate([-operand[..., middle:], operand[..., :middle]], axis=-1)

def head_attention(pieces):
    query_head, key_head, value_head = pieces
    scores = low_back(jnp.dot(query_head, key_head.T, precision=highest) * HEAD_DIM ** (-0.5))
    ordinal = jnp.arange(SEQ, dtype=jnp.int32)
    scores = jnp.where(ordinal[None, :] <= ordinal[:, None], scores, masked_score)
    highest_score = lax.optimization_barrier(jnp.max(scores, axis=1, keepdims=True))
    weights = jnp.exp(scores - highest_score)
    attention = weights / lax.optimization_barrier(jnp.sum(weights, axis=1, keepdims=True))
    return jnp.dot(low(attention), value_head, precision=highest)

def expert_rows(pieces):
    slot_rows, gate_matrix, up_matrix, down_matrix = pieces
    row_count = slot_rows.shape[0]
    group_width = FF // N_TENSOR
    repeated = low_back(jnp.broadcast_to(slot_rows[:, None, :], (row_count, N_TENSOR, D)))
    gate_pre = low_back(jnp.einsum('rnd,dnf->rnf', repeated, gate_matrix.reshape(D, N_TENSOR, group_width), precision=highest))
    up_pre = low_back(jnp.einsum('rnd,dnf->rnf', repeated, up_matrix.reshape(D, N_TENSOR, group_width), precision=highest))
    hidden = low(jax.nn.silu(gate_pre) * up_pre)
    pieces_out = jnp.einsum('rnf,nfd->rnd', hidden, down_matrix.reshape(N_TENSOR, group_width, D), precision=highest)
    return lax.optimization_barrier(jnp.sum(low(low_back(pieces_out)), axis=1))

def slot_tables(route_block):
    route_blocks = route_block.reshape(N_EXPERT, TOK_DEV * TOPK)
    one_hot = (route_blocks[:, :, None] == jnp.arange(EXPERTS, dtype=jnp.int32)[None, None, :]).astype(jnp.int32)
    earlier = jnp.cumsum(one_hot, axis=1) - one_hot
    ranking = lax.optimization_barrier(jnp.sum(earlier * one_hot, axis=2))
    source_idx = jnp.arange(N_EXPERT, dtype=jnp.int32)[:, None]
    placed = (route_blocks * N_EXPERT + source_idx) * CAP + ranking
    route_index = jnp.arange(SEQ * TOPK, dtype=jnp.int32)
    return jnp.full((EXPERTS * N_EXPERT * CAP,), -1, jnp.int32).at[placed.reshape(-1)].set(route_index)

def layer(source, params, route_block, cosine, sine, slot_table):
    norm1_gain, w_query, w_key, w_value, query_gain, key_gain, w_output, norm2_gain, w_router, w_gate, w_up, w_down = params
    shape_heads = (SEQ, HEADS, HEAD_DIM)
    norm_in = low(source * rms_scale(source) * norm1_gain)
    query_raw = low_back(jnp.dot(norm_in, w_query, precision=highest))
    key_raw = low_back(jnp.dot(norm_in, w_key, precision=highest))
    value_low = low(low_back(jnp.dot(norm_in, w_value, precision=highest)))
    query_normed = (query_raw * rms_scale(query_raw) * query_gain.reshape(D)).reshape(shape_heads)
    key_normed = (key_raw * rms_scale(key_raw) * key_gain.reshape(D)).reshape(shape_heads)
    query_turned = low(query_normed * cosine + turn_half(query_normed) * sine)
    key_turned = low(key_normed * cosine + turn_half(key_normed) * sine)
    heads_out = lax.map(jax.checkpoint(head_attention), (query_turned.transpose(1, 0, 2), key_turned.transpose(1, 0, 2), value_low.reshape(shape_heads).transpose(1, 0, 2)))
    attended = low(low_back(heads_out.transpose(1, 0, 2).reshape(SEQ, D)))
    residual = source + low_back(jnp.dot(attended, w_output, precision=highest))
    norm_out = low(residual * rms_scale(residual) * norm2_gain)
    router_probs = jax.nn.softmax(low_back(jnp.dot(norm_out, w_router, precision=highest)), axis=-1)
    gate_values = jnp.take_along_axis(router_probs, route_block, axis=1).reshape(-1)
    slot_filled = slot_table >= 0
    route_at = jnp.maximum(slot_table, 0)
    token_at = route_at // TOPK
    slot_rows = jnp.where(slot_filled[:, None], jnp.take(norm_out, token_at, axis=0), 0.0)
    results = lax.map(jax.checkpoint(expert_rows), (slot_rows.reshape(EXPERTS, N_EXPERT * CAP, D), w_gate, w_up, w_down))
    slot_gates = jnp.where(slot_filled, jnp.take(gate_values, route_at), 0.0)
    weighted = results.reshape(EXPERTS * N_EXPERT * CAP, D) * slot_gates[:, None]
    experts_out = jax.ops.segment_sum(weighted, token_at, num_segments=SEQ)
    return residual + experts_out

def reference(tokens, out_grad, routes, norm1_gain, w_query, w_key, w_value, query_gain, key_gain, w_output, norm2_gain, w_router, w_gate, w_up, w_down):
    params = tuple((item.astype(jnp.float32) for item in (norm1_gain, w_query, w_key, w_value, query_gain, key_gain, w_output, norm2_gain, w_router, w_gate, w_up, w_down)))
    frequency = theta_base ** (-(jnp.arange(HEAD_DIM // 2, dtype=jnp.float32) * 2.0 / HEAD_DIM))
    angles = jnp.arange(SEQ, dtype=jnp.float32)[:, None] * frequency[None, :]
    angles = jnp.concatenate([angles, angles], axis=1)
    cosine = jnp.cos(angles)[:, None, :]
    sine = jnp.sin(angles)[:, None, :]
    out_list = []
    input_list = []
    summed_grads = None
    for micro_idx in range(MB):
        route_block = routes[micro_idx]
        slot_table = slot_tables(route_block)

        def forward_fn(source, *weights):
            return layer(source, weights, route_block, cosine, sine, slot_table)
        result_out, pullback = jax.vjp(forward_fn, tokens[micro_idx].astype(jnp.float32), *params)
        gradients = pullback(out_grad[micro_idx].astype(jnp.float32))
        out_list.append(result_out.astype(jnp.bfloat16))
        input_list.append(gradients[0])
        if summed_grads is None:
            summed_grads = gradients[1:]
        else:
            summed_grads = tuple((first_term + next_term for first_term, next_term in zip(summed_grads, gradients[1:])))
    return (jnp.stack(out_list), jnp.stack(input_list), summed_grads[0], summed_grads[1], summed_grads[2], summed_grads[3], summed_grads[4], summed_grads[5], summed_grads[6], summed_grads[7], summed_grads[8], summed_grads[9], summed_grads[10], summed_grads[11])
```

```python
import jax
import jax.numpy as jnp
from jax import lax
from jax.sharding import PartitionSpec as P

eps = 1e-05
theta_base = 10000.0
masked_score = -1e30
bf16 = jnp.bfloat16
f32 = jnp.float32


def rms_scale(operand):
    return lax.rsqrt(jnp.mean(operand * operand, axis=-1, keepdims=True) + eps)


def turn_half(operand):
    middle = operand.shape[-1] // 2
    return jnp.concatenate([-operand[..., middle:], operand[..., :middle]], axis=-1)


def turn_back(operand):
    middle = operand.shape[-1] // 2
    return jnp.concatenate([operand[..., middle:], -operand[..., :middle]], axis=-1)


def bits_of(count):
    bits = []
    bit = count // 2
    while bit:
        bits.append(bit)
        bit //= 2
    return bits


def partner_order(bits):
    order = [0]
    for bit in bits:
        order = order + [place ^ bit for place in order]
    return order


def swap(operand, axis_name, bit):
    count = lax.axis_size(axis_name)
    return lax.ppermute(operand, axis_name, [(i, i ^ bit) for i in range(count)])


def double_rows(operand, steps, axis):
    for axis_name, bit in steps:
        operand = jnp.concatenate([operand, swap(operand, axis_name, bit)], axis=axis)
    return operand


def halve_rows(operand, steps, axis, last=bf16):
    for number, (axis_name, bit) in enumerate(steps):
        half = operand.shape[axis] // 2
        kept = lax.slice_in_dim(operand, 0, half, axis=axis)
        sent = lax.slice_in_dim(operand, half, 2 * half, axis=axis)
        total = kept.astype(f32) + swap(sent, axis_name, bit).astype(f32)
        operand = total if number == len(steps) - 1 and last == f32 else total.astype(bf16)
    return operand


def sum_over(operand, steps):
    for axis_name, bit in steps:
        operand = operand + swap(operand, axis_name, bit)
    return operand


def sum_over_rows(operand, steps, own_rows):
    shape = operand.shape
    blocked = operand.reshape((-1,) + (2,) * len(steps) + (own_rows,))
    for number, (axis_name, bit) in enumerate(steps):
        blocked = blocked + jnp.flip(swap(blocked, axis_name, bit), axis=len(steps) - number)
    return blocked.reshape(shape)


def mm(left, right):
    return jnp.dot(left, right, preferred_element_type=f32)


def mm_t(left, right):
    return lax.dot_general(left, right, (((1,), (1,)), ((), ())), preferred_element_type=f32)


def t_mm(left, right):
    return lax.dot_general(left, right, (((0,), (0,)), ((), ())), preferred_element_type=f32)


def attention_forward(query, key, value, causal, scale):
    scores = mm_t(query, key) * scale
    scores = jnp.where(causal, scores, masked_score)
    highest = jnp.max(scores, axis=1, keepdims=True)
    log_total = highest + jnp.log(jnp.sum(jnp.exp(scores - highest), axis=1, keepdims=True))
    probs_low = jnp.exp(scores - log_total).astype(bf16)
    return mm(probs_low, value).astype(bf16), log_total


def attention_backward(query, key, value, log_total, grad, causal, scale):
    scores = mm_t(query, key) * scale
    scores = jnp.where(causal, scores, masked_score)
    probs = jnp.exp(scores - log_total)
    probs_low = probs.astype(bf16)
    dprob = mm_t(grad, value)
    score_grad = (probs * (dprob - jnp.sum(dprob * probs, axis=1, keepdims=True))).astype(bf16)
    return (
        (mm(score_grad, key) * scale).astype(bf16),
        (t_mm(score_grad, query) * scale).astype(bf16),
        t_mm(probs_low, grad).astype(bf16),
    )


def shards(
    tokens,
    out_grad,
    routes,
    norm1_gain,
    w_query,
    w_key,
    w_value,
    query_gain,
    key_gain,
    w_output,
    norm2_gain,
    w_router,
    w_gate,
    w_up,
    w_down,
):
    micro_count, rows_here, width = tokens.shape
    local_width = w_query.shape[1]
    heads_here, head_size = query_gain.shape
    experts = w_router.shape[1]
    groups = lax.axis_size("expert")
    tensor_count = lax.axis_size("tensor")
    owned, _, hidden_width = w_gate.shape
    own_rows = rows_here // tensor_count
    flat_rows = micro_count * rows_here
    score_scale = head_size ** (-0.5)
    expert_at = lax.axis_index("expert")
    tensor_at = lax.axis_index("tensor")

    expert_bits = bits_of(groups)
    tensor_bits = bits_of(tensor_count)
    expert_steps = [("expert", bit) for bit in expert_bits]
    tensor_steps = [("tensor", bit) for bit in tensor_bits]
    all_steps = expert_steps + tensor_steps
    tensor_order = partner_order(tensor_bits)
    expert_order = partner_order(expert_bits)

    def by_partner(operand):
        return jnp.concatenate(
            [
                lax.dynamic_slice_in_dim(operand, (tensor_at ^ place) * own_rows, own_rows, axis=1)
                for place in tensor_order
            ],
            axis=1,
        )

    def in_sequence(operand):
        place_of = jnp.asarray(
            [tensor_order.index(place) for place in range(tensor_count)], jnp.int32
        )
        return jnp.concatenate(
            [
                lax.dynamic_slice_in_dim(
                    operand, place_of[tensor_at ^ place] * own_rows, own_rows, axis=1
                )
                for place in range(tensor_count)
            ],
            axis=1,
        )

    def columns_by_partner(operand):
        block = operand.shape[1] // groups
        return jnp.concatenate(
            [
                lax.dynamic_slice_in_dim(operand, (expert_at ^ place) * block, block, axis=1)
                for place in expert_order
            ],
            axis=1,
        )

    pairs = micro_count * heads_here
    per_device = max(1, pairs // groups)
    copies = max(1, groups // pairs)

    def to_heads(operand):
        wide = operand.shape[3]
        blocks = operand.transpose(0, 2, 1, 3).reshape(pairs, rows_here, wide)
        if copies > 1:
            blocks = jnp.repeat(blocks, copies, axis=0)
        blocks = lax.all_to_all(blocks, "expert", split_axis=0, concat_axis=0, tiled=True)
        blocks = blocks.reshape(groups, per_device, rows_here, wide)
        return blocks.transpose(1, 0, 2, 3).reshape(per_device, groups * rows_here, wide)

    def from_heads(operand):
        wide = operand.shape[2]
        blocks = operand.reshape(per_device, groups, rows_here, wide).transpose(1, 0, 2, 3)
        blocks = blocks.reshape(groups * per_device, rows_here, wide)
        blocks = lax.all_to_all(blocks, "expert", split_axis=0, concat_axis=0, tiled=True)
        if copies > 1:
            blocks = blocks[::copies]
        return blocks.reshape(micro_count, heads_here, rows_here, wide).transpose(0, 2, 1, 3)

    row_number = jnp.arange(own_rows, dtype=jnp.int32)
    row_in_block = jnp.concatenate(
        [(tensor_at ^ place) * own_rows + row_number for place in tensor_order]
    )
    row_pos = expert_at * rows_here + row_in_block
    frequency = theta_base ** (-(jnp.arange(head_size // 2, dtype=f32) * 2.0 / head_size))
    angles = row_pos.astype(f32)[:, None] * frequency[None, :]
    angles = jnp.concatenate([angles, angles], axis=1)
    cosine = jnp.cos(angles)[:, None, :]
    sine = jnp.sin(angles)[:, None, :]
    sequence_pos = (
        jnp.arange(groups, dtype=jnp.int32)[:, None] * rows_here + row_in_block[None, :]
    ).reshape(-1)
    causal = sequence_pos[None, :] <= sequence_pos[:, None]

    grad_rows = lax.dynamic_slice_in_dim(out_grad, tensor_at * own_rows, own_rows, axis=1)
    route_rows = lax.dynamic_slice_in_dim(routes, tensor_at * own_rows, own_rows, axis=1)
    mask_rows = jnp.sum(
        (route_rows[..., None] == jnp.arange(experts, dtype=jnp.int32)).astype(f32), axis=2
    )
    mask_all = double_rows(mask_rows.astype(bf16), all_steps, 1)
    upstream_all = [double_rows(grad_rows[m], all_steps, 0) for m in range(micro_count)]

    source = by_partner(tokens).astype(f32)
    scale_in = rms_scale(source)
    norm_in = (source * scale_in * norm1_gain).astype(bf16).reshape(flat_rows, width)
    query_raw = mm(norm_in, w_query)
    key_raw = mm(norm_in, w_key)
    value_low = mm(norm_in, w_value).astype(bf16)
    squares = jnp.stack([jnp.sum(query_raw * query_raw, axis=1), jnp.sum(key_raw * key_raw, axis=1)])
    squares = sum_over_rows(squares, tensor_steps, own_rows)
    query_scale = lax.rsqrt(squares[0] / width + eps)[:, None]
    key_scale = lax.rsqrt(squares[1] / width + eps)[:, None]
    query_gain_flat = query_gain.reshape(local_width)
    key_gain_flat = key_gain.reshape(local_width)
    head_shape = (micro_count, rows_here, heads_here, head_size)

    def turned(raw, scale, gain):
        normed = (raw * scale * gain).reshape(head_shape)
        return (normed * cosine + turn_half(normed) * sine).astype(bf16)

    packed = jnp.concatenate(
        [
            turned(query_raw, query_scale, query_gain_flat),
            turned(key_raw, key_scale, key_gain_flat),
            value_low.reshape(head_shape),
        ],
        axis=3,
    )
    packed = to_heads(packed)
    head_parts = []
    for number in range(per_device):
        parts = [
            packed[number, :, part * head_size : (part + 1) * head_size] for part in range(3)
        ]
        head_parts.append((parts, attention_forward(*parts, causal, score_scale)))
    attended = from_heads(jnp.stack([out for _, (out, _) in head_parts]))
    attended = attended.reshape(flat_rows, local_width)

    attn_part = mm(attended, w_output).astype(bf16).reshape(micro_count, rows_here, width)
    attn_rows = halve_rows(attn_part, tensor_steps[::-1], 1, f32)
    own_source = source[:, :own_rows]
    residual = own_source + attn_rows
    scale_out = rms_scale(residual)
    norm_out = (residual * scale_out * norm2_gain).astype(bf16)
    flat_out = norm_out.reshape(micro_count * own_rows, width)
    router_probs = jax.nn.softmax(mm(flat_out, w_router), axis=-1).reshape(
        micro_count, own_rows, experts
    )

    expert_base = expert_at * owned
    gathered = []
    out_rows = []
    row_grads = []
    prob_grads = []
    for m in range(micro_count):
        rows_all = double_rows(norm_out[m], all_steps, 0)
        probs_all = jax.nn.softmax(mm(rows_all, w_router), axis=-1) * mask_all[m].astype(f32)
        gates = lax.dynamic_slice_in_dim(probs_all, expert_base, owned, axis=1)[:, :, None]
        gate_pre = jnp.einsum("td,edf->tef", rows_all, w_gate, preferred_element_type=f32)
        up_pre = jnp.einsum("td,edf->tef", rows_all, w_up, preferred_element_type=f32)
        back = jnp.einsum("td,efd->tef", upstream_all[m], w_down, preferred_element_type=f32)
        sigmoid_gate = jax.nn.sigmoid(gate_pre)
        activated = gate_pre * sigmoid_gate
        hidden = activated * up_pre
        gated_hidden = (gates * hidden).astype(bf16)
        out_part = jnp.einsum(
            "tef,efd->td", gated_hidden, w_down, preferred_element_type=f32
        ).astype(bf16)
        gate_grad = jnp.sum(hidden * back, axis=2)
        hidden_grad = gates * back
        gate_back = (
            hidden_grad * up_pre * (sigmoid_gate * (1.0 + gate_pre * (1.0 - sigmoid_gate)))
        ).astype(bf16)
        up_back = (hidden_grad * activated).astype(bf16)
        row_part = (
            jnp.einsum("tef,edf->td", gate_back, w_gate, preferred_element_type=f32)
            + jnp.einsum("tef,edf->td", up_back, w_up, preferred_element_type=f32)
        ).astype(bf16)
        gathered.append((rows_all, upstream_all[m], gated_hidden, gate_back, up_back))
        row_grads.append(halve_rows(row_part, all_steps[::-1], 0, f32))
        spread = lax.dynamic_update_slice_in_dim(
            jnp.zeros((gate_grad.shape[0], experts), bf16), gate_grad.astype(bf16), expert_base, 1
        )
        prob_grads.append(halve_rows(spread, all_steps[::-1], 0, f32))
        out_rows.append(halve_rows(out_part, all_steps[::-1], 0, f32))
    grad_gate = sum(
        jnp.einsum("td,tef->edf", item[0], item[3], preferred_element_type=f32)
        for item in gathered
    )
    grad_up = sum(
        jnp.einsum("td,tef->edf", item[0], item[4], preferred_element_type=f32)
        for item in gathered
    )
    grad_down = sum(
        jnp.einsum("tef,td->efd", item[2], item[1], preferred_element_type=f32)
        for item in gathered
    )
    layer_out = (residual + jnp.stack(out_rows)).astype(bf16)
    layer_out = lax.all_to_all(layer_out, "tensor", split_axis=2, concat_axis=1, tiled=True)

    prob_grad = jnp.stack(prob_grads) * mask_rows
    logit_grad = (
        router_probs * (prob_grad - jnp.sum(prob_grad * router_probs, axis=2, keepdims=True))
    ).astype(bf16)
    flat_logit = logit_grad.reshape(micro_count * own_rows, experts)
    norm_out_grad = jnp.stack(row_grads) + mm_t(flat_logit, w_router).reshape(residual.shape)
    router_part = t_mm(flat_logit, flat_out)
    second_gain_part = jnp.sum(norm_out_grad * residual * scale_out, axis=(0, 1))
    weighted_out = norm_out_grad * norm2_gain
    residual_grad = (
        grad_rows.astype(f32)
        + scale_out * weighted_out
        - residual * scale_out**3 * jnp.mean(weighted_out * residual, axis=2, keepdims=True)
    )
    residual_low = double_rows(residual_grad.astype(bf16), tensor_steps, 1).reshape(
        flat_rows, width
    )

    first_step, later_steps = expert_steps[-1], expert_steps[:-1][::-1]

    def pair_left(operand):
        wide = columns_by_partner(operand)
        half = wide.shape[1] // 2
        return jnp.concatenate([wide[:, :half], swap(wide[:, half:], *first_step)], axis=0)

    def pair_right(operand):
        return jnp.concatenate([operand, swap(operand, *first_step)], axis=0)

    def weight_grad(left_pair, right_pair):
        return halve_rows(t_mm(left_pair, right_pair).astype(bf16), later_steps, 0, f32)

    norm_in_pair = pair_left(norm_in)
    attended_pair = pair_right(attended)
    grad_output = weight_grad(pair_left(residual_low), attended_pair).T

    attended_grad = mm_t(residual_low, w_output).astype(bf16).reshape(head_shape)
    attended_grad = to_heads(attended_grad)
    head_grads = []
    for number in range(per_device):
        parts, (_, log_total) = head_parts[number]
        grads = attention_backward(*parts, log_total, attended_grad[number], causal, score_scale)
        head_grads.append(jnp.concatenate(grads, axis=1))
    packed_grad = from_heads(jnp.stack(head_grads))
    value_grad_low = packed_grad[..., 2 * head_size :].reshape(flat_rows, local_width)

    def turned_back(grad):
        grad = grad.astype(f32)
        return (grad * cosine + turn_back(grad * sine)).reshape(flat_rows, local_width)

    normed_q_grad = turned_back(packed_grad[..., :head_size])
    normed_k_grad = turned_back(packed_grad[..., head_size : 2 * head_size])
    row_dots = jnp.stack(
        [
            jnp.sum(normed_q_grad * query_gain_flat * query_raw, axis=1),
            jnp.sum(normed_k_grad * key_gain_flat * key_raw, axis=1),
        ]
    )
    row_dots = sum_over_rows(row_dots, tensor_steps, own_rows)
    query_gain_part = jnp.sum(normed_q_grad * query_raw * query_scale, axis=0)
    key_gain_part = jnp.sum(normed_k_grad * key_raw * key_scale, axis=0)
    query_grad_low = (
        query_scale * query_gain_flat * normed_q_grad
        - query_raw * query_scale**3 * row_dots[0][:, None] / width
    ).astype(bf16)
    key_grad_low = (
        key_scale * key_gain_flat * normed_k_grad
        - key_raw * key_scale**3 * row_dots[1][:, None] / width
    ).astype(bf16)
    grad_value = weight_grad(norm_in_pair, pair_right(value_grad_low))
    grad_query = weight_grad(norm_in_pair, pair_right(query_grad_low))
    grad_key = weight_grad(norm_in_pair, pair_right(key_grad_low))
    norm_in_part = (
        mm_t(query_grad_low, w_query) + mm_t(key_grad_low, w_key) + mm_t(value_grad_low, w_value)
    )
    norm_in_grad = halve_rows(
        norm_in_part.astype(bf16).reshape(micro_count, rows_here, width),
        tensor_steps[::-1],
        1,
        f32,
    )
    own_scale = scale_in[:, :own_rows]
    first_gain_part = jnp.sum(norm_in_grad * own_source * own_scale, axis=(0, 1))
    weighted_in = norm_in_grad * norm1_gain
    tokens_grad = (
        residual_grad
        + own_scale * weighted_in
        - own_source * own_scale**3 * jnp.mean(weighted_in * own_source, axis=2, keepdims=True)
    )
    tokens_grad = in_sequence(double_rows(tokens_grad.astype(bf16), tensor_steps, 1)).astype(f32)

    head_block = head_size // groups
    head_gains = jnp.stack([query_gain_part, key_gain_part]).reshape(
        2 * heads_here, groups, head_block
    )
    head_gains = head_gains.transpose(1, 0, 2).reshape(groups, 2 * heads_here * head_block)
    column_block = width // groups
    head_gains = jnp.pad(head_gains, ((0, 0), (0, column_block - head_gains.shape[1])))
    head_rows = jnp.where(
        jnp.arange(tensor_count, dtype=jnp.int32)[:, None] == tensor_at,
        head_gains.reshape(1, width),
        0.0,
    )
    small = jnp.concatenate(
        [router_part, first_gain_part[None], second_gain_part[None], head_rows], axis=0
    )
    padding = -small.shape[0] % 16
    small = jnp.pad(small, ((0, padding), (0, 0))).astype(bf16)
    small = columns_by_partner(small)
    small = halve_rows(small, expert_steps[::-1], 1)
    small = sum_over(small, tensor_steps).astype(f32)
    grad_router = small[:experts].T
    own_heads = lax.dynamic_slice_in_dim(small, experts + 2 + tensor_at, 1, axis=0)
    own_heads = own_heads[0, : 2 * heads_here * head_block].reshape(2, heads_here, head_block)
    return (
        layer_out,
        tokens_grad,
        small[experts],
        grad_query,
        grad_key,
        grad_value,
        own_heads[0],
        own_heads[1],
        grad_output,
        small[experts + 1],
        grad_router,
        grad_gate,
        grad_up,
        grad_down,
    )


def solution(mesh):
    placed = (
        P(None, "expert", None),
        P(None, "expert", None),
        P(None, "expert", None),
        P(),
        P(None, "tensor"),
        P(None, "tensor"),
        P(None, "tensor"),
        P("tensor", None),
        P("tensor", None),
        P("tensor", None),
        P(),
        P(),
        P("expert", None, "tensor"),
        P("expert", None, "tensor"),
        P("expert", "tensor", None),
    )
    return jax.shard_map(
        shards,
        mesh=mesh,
        in_specs=placed,
        out_specs=(
            P(None, "expert", "tensor"),
            P(None, "expert", None),
            P("expert"),
            P("expert", "tensor"),
            P("expert", "tensor"),
            P("expert", "tensor"),
            P("tensor", "expert"),
            P("tensor", "expert"),
            P("tensor", "expert"),
            P("expert"),
            P("expert", None),
            P("expert", None, "tensor"),
            P("expert", None, "tensor"),
            P("expert", "tensor", None),
        ),
        check_vma=False,
    )
```

```python
import functools

import jax
import jax.numpy as jnp
from jax import lax
from jax.experimental import pallas as pl
from jax.experimental.pallas import tpu as pltpu
from jax.sharding import PartitionSpec as P

eps = 1e-05
theta_base = 10000.0
masked_score = -1e30
bf16 = jnp.bfloat16
f32 = jnp.float32
vmem_limit = 56 * 1024 * 1024
expert_rows_most = 1024


def rms_scale(operand):
    return lax.rsqrt(jnp.mean(operand * operand, axis=-1, keepdims=True) + eps)


def turn_half(operand):
    middle = operand.shape[-1] // 2
    return jnp.concatenate([-operand[..., middle:], operand[..., :middle]], axis=-1)


def turn_back(operand):
    middle = operand.shape[-1] // 2
    return jnp.concatenate([operand[..., middle:], -operand[..., :middle]], axis=-1)


def bits_of(count):
    bits = []
    bit = count // 2
    while bit:
        bits.append(bit)
        bit //= 2
    return bits


def partner_order(bits):
    order = [0]
    for bit in bits:
        order = order + [place ^ bit for place in order]
    return order


def swap(operand, axis_name, bit):
    count = lax.axis_size(axis_name)
    return lax.ppermute(operand, axis_name, [(i, i ^ bit) for i in range(count)])


def double_rows(operand, steps, axis):
    for axis_name, bit in steps:
        operand = jnp.concatenate([operand, swap(operand, axis_name, bit)], axis=axis)
    return operand


def halve_rows(operand, steps, axis, last=bf16):
    for number, (axis_name, bit) in enumerate(steps):
        half = operand.shape[axis] // 2
        kept = lax.slice_in_dim(operand, 0, half, axis=axis)
        sent = lax.slice_in_dim(operand, half, 2 * half, axis=axis)
        total = kept.astype(f32) + swap(sent, axis_name, bit).astype(f32)
        operand = total if number == len(steps) - 1 and last == f32 else total.astype(bf16)
    return operand


def sum_over(operand, steps):
    for axis_name, bit in steps:
        operand = operand + swap(operand, axis_name, bit)
    return operand


def sum_over_rows(operand, steps, own_rows):
    shape = operand.shape
    blocked = operand.reshape((-1,) + (2,) * len(steps) + (own_rows,))
    for number, (axis_name, bit) in enumerate(steps):
        blocked = blocked + jnp.flip(swap(blocked, axis_name, bit), axis=len(steps) - number)
    return blocked.reshape(shape)


def mm(left, right):
    return jnp.dot(left, right, preferred_element_type=f32)


def mm_t(left, right):
    return lax.dot_general(left, right, (((1,), (1,)), ((), ())), preferred_element_type=f32)


def t_mm(left, right):
    return lax.dot_general(left, right, (((0,), (0,)), ((), ())), preferred_element_type=f32)


def after(operand, *others):
    def nothing(*refs):
        pass

    anywhere = pl.BlockSpec(memory_space=pl.ANY)
    return pl.pallas_call(
        nothing,
        out_shape=jax.ShapeDtypeStruct(operand.shape, operand.dtype),
        in_specs=[anywhere] * (1 + len(others)),
        out_specs=anywhere,
        input_output_aliases={0: 0},
    )(operand, *others)


def after_all(operands, *others):
    return [after(operand, *others) for operand in operands] if others else list(operands)


def upstream_kernel(place, blocks, width, table_ref, down_ref, gathered_ref, *refs):
    back_ref, mask_ref, rows_ref, sems = refs[-4:]
    own_rows = rows_ref.shape[0] // blocks

    @pl.when(pl.program_id(0) == 0)
    def _():
        copies = []
        for number in range(blocks):
            start = pl.multiple_of(table_ref[place * blocks + number] * own_rows, own_rows)
            source = gathered_ref.at[pl.ds(start, own_rows)]
            there = pl.ds(number * own_rows, own_rows)
            copies.append(
                pltpu.make_async_copy(
                    source.at[:, pl.ds(0, width)], rows_ref.at[there], sems.at[0, number]
                )
            )
            copies.append(
                pltpu.make_async_copy(
                    source.at[:, pl.ds(width, 128)], mask_ref.at[there], sems.at[1, number]
                )
            )
        for copy in copies:
            copy.start()
        for copy in copies:
            copy.wait()

    back_ref[...] = mm_t(rows_ref[...], down_ref[0])


def upstream_products(place, calls, table, gathered, w_down, kept, tokens):
    owned, hidden_width, width = w_down.shape
    blocks = table.shape[0] // calls
    rows = gathered.shape[0] // calls
    anywhere = pl.BlockSpec(memory_space=pl.ANY)
    others = [gathered] + kept + tokens
    return pl.pallas_call(
        functools.partial(upstream_kernel, place, blocks, width),
        out_shape=[
            jax.ShapeDtypeStruct((rows, owned * hidden_width), f32),
            jax.ShapeDtypeStruct((rows, 128), bf16),
            jax.ShapeDtypeStruct((calls * rows, width), bf16),
        ],
        grid_spec=pltpu.PrefetchScalarGridSpec(
            num_scalar_prefetch=1,
            grid=(owned,),
            in_specs=[pl.BlockSpec((1, hidden_width, width), lambda step, table: (step, 0, 0))]
            + [anywhere] * len(others),
            out_specs=[
                pl.BlockSpec((rows, hidden_width), lambda step, table: (0, step)),
                pl.BlockSpec((rows, 128), lambda step, table: (0, 0)),
                pl.BlockSpec((rows, width), lambda step, table: (place, 0)),
            ],
            scratch_shapes=[pltpu.SemaphoreType.DMA((2, blocks))],
        ),
        input_output_aliases={3: 2} if kept else {},
        compiler_params=pltpu.CompilerParams(vmem_limit_bytes=vmem_limit),
        cost_estimate=pl.CostEstimate(
            flops=2 * rows * width * owned * hidden_width,
            bytes_accessed=8 * rows * width,
            transcendentals=0,
        ),
    )(table, w_down, *others)


def expert_kernel(
    plan, copy_count, width, base_ref, mask_ref, router_ref, gate_ref, up_ref, back_ref, *refs
):
    piece_count = sum(len(block) for block in plan)
    piece_refs = refs[:piece_count]
    part_refs = refs[-11 - copy_count : -11]
    copy_ref, gated_ref, gate_back_ref, up_back_ref = refs[-11:-7]
    rows, gates, ups, probs, row_sems, gate_sems, up_sems = refs[-7:]
    step = pl.program_id(0)
    experts = router_ref.shape[1]
    owned, _, hidden_width = gate_ref.shape

    def row_copies(block):
        copies, start = [], 0
        first = sum(len(item) for item in plan[:block])
        for number in range(len(plan[block])):
            piece_ref = piece_refs[first + number]
            count = piece_ref.shape[0]
            copies.append(
                pltpu.make_async_copy(
                    piece_ref,
                    rows.at[block % 2, pl.ds(start, count)],
                    row_sems.at[block % 2, number],
                )
            )
            start += count
        return copies

    def weight_copies(number):
        here = pl.ds(number * hidden_width, hidden_width)
        return [
            pltpu.make_async_copy(gate_ref.at[number], gates.at[:, here], gate_sems.at[number]),
            pltpu.make_async_copy(up_ref.at[number], ups.at[:, here], up_sems.at[number]),
        ]

    @pl.when(step == 0)
    def _():
        for copy in row_copies(0):
            copy.start()
        for number in range(owned):
            for copy in weight_copies(number):
                copy.start()

    for block in range(len(plan)):

        @pl.when(step == block)
        def _(block=block):
            for copy in row_copies(block):
                copy.wait()
            if block + 1 < len(plan):
                for copy in row_copies(block + 1):
                    copy.start()

    own_rows = rows[step % 2]
    copy_ref[...] = own_rows
    logits = mm(own_rows, router_ref[...])
    weights = jnp.exp(logits - jnp.max(logits, axis=1, keepdims=True))
    weights = weights / jnp.sum(weights, axis=1, keepdims=True)
    probs[...] = weights * mask_ref[:, :experts].astype(f32)
    lane = lax.broadcasted_iota(jnp.int32, probs.shape, 1)
    slope_lane = lax.broadcasted_iota(jnp.int32, (own_rows.shape[0], 128), 1)

    slopes = jnp.zeros(slope_lane.shape, f32)
    for number in range(owned):
        here = slice(number * hidden_width, (number + 1) * hidden_width)
        owner = base_ref[0] + number

        @pl.when(step == 0)
        def _(number=number):
            for copy in weight_copies(number):
                copy.wait()

        gate = jnp.sum(jnp.where(lane == owner, probs[...], 0.0), axis=1, keepdims=True)
        gate_pre = mm(rows[step % 2], gates[:, here])
        up_pre = mm(rows[step % 2], ups[:, here])
        back = back_ref[:, here]
        sigmoid_gate = 1.0 / (1.0 + jnp.exp(-gate_pre))
        activated = gate_pre * sigmoid_gate
        hidden = activated * up_pre
        gated_ref[:, here] = (gate * hidden).astype(bf16)
        slope = jnp.sum(hidden * back, axis=1, keepdims=True)
        slopes = slopes + jnp.where(slope_lane == owner, slope, 0.0)
        hidden_grad = gate * back
        gate_back_ref[:, here] = (
            hidden_grad * up_pre * (sigmoid_gate * (1.0 + gate_pre * (1.0 - sigmoid_gate)))
        ).astype(bf16)
        up_back_ref[:, here] = (hidden_grad * activated).astype(bf16)
    part = mm_t(gate_back_ref[...], gates[...]) + mm_t(up_back_ref[...], ups[...])
    part = part.astype(bf16)
    per_copy = len(plan) // copy_count
    for copy, part_ref in enumerate(part_refs):

        @pl.when(step // per_copy == copy)
        def _(part_ref=part_ref):
            part_ref[:, :width] = part
            part_ref[:, width:] = slopes.astype(bf16)


def expert_call(
    place, total_rows, part, base, copies, block_rows, mask, router, w_gate, w_up, back, kept
):
    plan, pieces = [], []
    for copy in copies:
        for piece in copy:
            if not plan or sum(item.shape[0] for item in plan[-1]) == block_rows:
                plan.append([])
            plan[-1].append(piece)
            pieces.append(piece)
    copy_count = len(copies)
    per_copy = len(plan) // copy_count
    owned, width, hidden_width = w_gate.shape
    hidden = owned * hidden_width
    experts = router.shape[1]
    blocks = len(plan)
    anywhere = pl.BlockSpec(memory_space=pl.ANY)
    here = lambda step, base_ref: (place * blocks + step, 0)
    in_specs = [
        pl.BlockSpec((block_rows, 128), lambda step, base_ref: (part * blocks + step, 0)),
        pl.BlockSpec((width, experts), lambda step, base_ref: (0, 0)),
        anywhere,
        anywhere,
        pl.BlockSpec((block_rows, hidden), lambda step, base_ref: (part * blocks + step, 0)),
    ] + [anywhere] * len(pieces)

    def part_block(copy):
        return pl.BlockSpec(
            (block_rows, width + 128),
            lambda step, base_ref: (jnp.clip(step - copy * per_copy, 0, per_copy - 1), 0),
        )

    out_specs = [part_block(copy) for copy in range(copy_count)] + [
        pl.BlockSpec((block_rows, width), here),
        pl.BlockSpec((block_rows, hidden), here),
        pl.BlockSpec((block_rows, hidden), here),
        pl.BlockSpec((block_rows, hidden), here),
    ]
    hidden_shape = jax.ShapeDtypeStruct((total_rows, hidden), bf16)
    out_shape = [
        jax.ShapeDtypeStruct((per_copy * block_rows, width + 128), bf16)
    ] * copy_count + [
        jax.ShapeDtypeStruct((total_rows, width), bf16),
        hidden_shape,
        hidden_shape,
        hidden_shape,
    ]
    aliases = {}
    if kept:
        aliases = {
            1 + len(in_specs) + number: copy_count + number for number in range(len(kept))
        }
    in_specs += [anywhere] * len(kept)
    most_pieces = max(len(block) for block in plan)
    count = blocks * block_rows
    outs = pl.pallas_call(
        functools.partial(expert_kernel, plan, copy_count, width),
        out_shape=out_shape,
        grid_spec=pltpu.PrefetchScalarGridSpec(
            num_scalar_prefetch=1,
            grid=(blocks,),
            in_specs=in_specs,
            out_specs=out_specs,
            scratch_shapes=[
                pltpu.VMEM((2, block_rows, width), bf16),
                pltpu.VMEM((width, hidden), bf16),
                pltpu.VMEM((width, hidden), bf16),
                pltpu.VMEM((block_rows, experts), f32),
                pltpu.SemaphoreType.DMA((2, most_pieces)),
                pltpu.SemaphoreType.DMA((owned,)),
                pltpu.SemaphoreType.DMA((owned,)),
            ],
        ),
        input_output_aliases=aliases,
        compiler_params=pltpu.CompilerParams(vmem_limit_bytes=vmem_limit),
        cost_estimate=pl.CostEstimate(
            flops=8 * count * width * hidden,
            bytes_accessed=4 * width * hidden + 8 * count * width,
            transcendentals=count * hidden,
        ),
    )(base, mask, router, w_gate, w_up, back, *pieces, *kept)
    return list(outs[:copy_count]), list(outs[copy_count:])


def down_kernel(copy_count, gated_ref, down_ref, *refs):
    total = None
    for number in range(down_ref.shape[0]):
        hidden_width = down_ref.shape[1]
        here = slice(number * hidden_width, (number + 1) * hidden_width)
        part = mm(gated_ref[:, here], down_ref[number])
        total = part if total is None else total + part
    for copy, out_ref in enumerate(refs[-copy_count:]):

        @pl.when(pl.program_id(0) == copy)
        def _(out_ref=out_ref):
            out_ref[...] = total.astype(bf16)


def down_products(place, calls, copy_count, gated, w_down, tokens):
    owned, hidden_width, width = w_down.shape
    block = gated.shape[0] // (calls * copy_count)
    return pl.pallas_call(
        functools.partial(down_kernel, copy_count),
        out_shape=[jax.ShapeDtypeStruct((block, width), bf16)] * copy_count,
        grid=(copy_count,),
        in_specs=[
            pl.BlockSpec(
                (block, owned * hidden_width), lambda step: (place * copy_count + step, 0)
            ),
            pl.BlockSpec((owned, hidden_width, width), lambda step: (0, 0, 0)),
        ]
        + [pl.BlockSpec(memory_space=pl.ANY)] * len(tokens),
        out_specs=[pl.BlockSpec((block, width), lambda step: (0, 0))] * copy_count,
        compiler_params=pltpu.CompilerParams(vmem_limit_bytes=vmem_limit),
        cost_estimate=pl.CostEstimate(
            flops=2 * block * copy_count * width * owned * hidden_width,
            bytes_accessed=4 * block * copy_count * width,
            transcendentals=0,
        ),
    )(gated, w_down, *tokens)


def product_kernel(left_ref, right_ref, *refs):
    refs[-1][0] = t_mm(left_ref[...], right_ref[...])


def expert_grads(left, right, owned, tokens):
    total_rows = left.shape[0]
    whole = lambda count: pl.BlockSpec(
        (total_rows, count), lambda step: (0, 0), pipeline_mode=pl.Buffered(1)
    )
    cut = lambda count: pl.BlockSpec((total_rows, count), lambda step: (0, step))
    if left.shape[1] > right.shape[1]:
        out = (left.shape[1], right.shape[1] // owned)
        specs = [whole(out[0]), cut(out[1])]
    else:
        out = (left.shape[1] // owned, right.shape[1])
        specs = [cut(out[0]), whole(out[1])]
    return pl.pallas_call(
        product_kernel,
        grid=(owned,),
        out_shape=jax.ShapeDtypeStruct((owned,) + out, f32),
        in_specs=specs + [pl.BlockSpec(memory_space=pl.ANY)] * len(tokens),
        out_specs=pl.BlockSpec((1,) + out, lambda step: (step, 0, 0)),
        compiler_params=pltpu.CompilerParams(vmem_limit_bytes=vmem_limit),
        cost_estimate=pl.CostEstimate(
            flops=2 * total_rows * owned * out[0] * out[1],
            bytes_accessed=4 * owned * out[0] * out[1] + 4 * total_rows * max(out),
            transcendentals=0,
        ),
    )(left, right, *tokens)


def kernel_params():
    return pltpu.CompilerParams(vmem_limit_bytes=vmem_limit)


def in_vmem(count):
    return [pl.BlockSpec(memory_space=pltpu.VMEM)] * count


def as_row(columns):
    return columns.T[:8]


def as_columns(rows):
    count = rows.shape[1]
    return jnp.concatenate([rows, jnp.zeros((120, count), rows.dtype)], axis=0).T


def in_lanes(*columns):
    lane = lax.broadcasted_iota(jnp.int32, (columns[0].shape[0], 128), 1)
    total = jnp.zeros(lane.shape, f32)
    for number, column in enumerate(columns):
        total = jnp.where(lane == number, column, total)
    return total


def summed_rows(own_ref, arrived_refs, own_rows):
    total = as_columns(own_ref[...])
    count = total.shape[0] // own_rows
    places = len(arrived_refs) + 1
    for place, arrived_ref in enumerate(arrived_refs, 1):
        arrived = as_columns(arrived_ref[...])
        blocks = [
            arrived[other * own_rows : (other + 1) * own_rows]
            for other in ((block // places) * places + ((block % places) ^ place) for block in range(count))
        ]
        total = total + jnp.concatenate(blocks, axis=0)
    return total


def project_kernel(
    rows_ref, gain_ref, query_ref, key_ref, value_ref, normed_ref, q_ref, k_ref, v_ref, squares_ref, sums
):
    step = pl.program_id(0)

    @pl.when(step == 0)
    def _():
        rows = rows_ref[...].astype(f32)
        normed_ref[...] = (rows * rms_scale(rows) * gain_ref[...]).astype(bf16)

    normed = normed_ref[...]
    query, key = mm(normed, query_ref[...]), mm(normed, key_ref[...])
    q_ref[...] = query
    k_ref[...] = key
    v_ref[...] = mm(normed, value_ref[...]).astype(bf16)
    here = in_lanes(
        jnp.sum(query * query, axis=1, keepdims=True), jnp.sum(key * key, axis=1, keepdims=True)
    )
    sums[...] = jnp.where(step == 0, 0.0, sums[...]) + here
    squares_ref[...] = as_row(sums[...])


def project(rows, gain, w_query, w_key, w_value):
    count, width = rows.shape
    local_width = w_query.shape[1]
    block = min(256, local_width)
    weight = pl.BlockSpec((width, block), lambda step: (0, step))
    whole = lambda *shape: pl.BlockSpec(shape, lambda step: (0, 0))
    out = pl.BlockSpec((count, block), lambda step: (0, step))
    raw = jax.ShapeDtypeStruct((count, local_width), f32)
    return pl.pallas_call(
        project_kernel,
        grid=(local_width // block,),
        out_shape=[
            jax.ShapeDtypeStruct((count, width), bf16),
            raw,
            raw,
            jax.ShapeDtypeStruct((count, local_width), bf16),
            jax.ShapeDtypeStruct((8, count), f32),
        ],
        in_specs=[whole(count, width), whole(1, width), weight, weight, weight],
        out_specs=[whole(count, width), out, out, out, whole(8, count)],
        scratch_shapes=[pltpu.VMEM((count, 128), f32)],
        compiler_params=kernel_params(),
    )(rows, gain[None], w_query, w_key, w_value)


def turn_kernel(
    own_rows, width, partners, q_ref, k_ref, v_ref, q_gain_ref, k_gain_ref, cos_ref, sin_ref, own_ref, *refs
):
    packed_ref, scales_ref = refs[partners:]
    squares = summed_rows(own_ref, refs[:partners], own_rows)
    scales = lax.rsqrt(squares / width + eps)
    scales_ref[...] = scales
    pairs, rows, wide = packed_ref.shape
    size = wide // 3
    heads = q_ref.shape[1] // size
    for pair in range(pairs):
        micro, head = pair // heads, pair % heads
        here = slice(micro * rows, (micro + 1) * rows)
        lanes = slice(head * size, (head + 1) * size)
        for part, (raw_ref, gain_ref) in enumerate(((q_ref, q_gain_ref), (k_ref, k_gain_ref))):
            normed = raw_ref[here, lanes] * scales[here, part : part + 1] * gain_ref[:, lanes]
            turned = normed * cos_ref[...] + turn_half(normed) * sin_ref[...]
            packed_ref[pair, :, part * size : (part + 1) * size] = turned.astype(bf16)
        packed_ref[pair, :, 2 * size :] = v_ref[here, lanes]


def turn_and_pack(query, key, value, gains, cosine, sine, squares, arrived, own_rows, width, pairs):
    rows, size = cosine.shape
    count = query.shape[0]
    return pl.pallas_call(
        functools.partial(turn_kernel, own_rows, width, len(arrived)),
        out_shape=[
            jax.ShapeDtypeStruct((pairs, rows, 3 * size), bf16),
            jax.ShapeDtypeStruct((count, 128), f32),
        ],
        in_specs=in_vmem(8 + len(arrived)),
        out_specs=in_vmem(2),
        compiler_params=kernel_params(),
    )(query, key, value, *gains, cosine, sine, squares, *arrived)


def unturn_kernel(
    packed_ref, q_ref, k_ref, q_gain_ref, k_gain_ref, cos_ref, sin_ref, scales_ref,
    q_grad_ref, k_grad_ref, v_grad_ref, dots_ref, gains_ref,
):
    pairs, rows, wide = packed_ref.shape
    size = wide // 3
    heads = q_ref.shape[1] // size
    gains_ref[...] = jnp.zeros_like(gains_ref)
    dots = []
    for micro in range(pairs // heads):
        here = slice(micro * rows, (micro + 1) * rows)
        sums = [jnp.zeros((rows, 1), f32)] * 2
        for head in range(heads):
            lanes = slice(head * size, (head + 1) * size)
            refs = ((q_ref, q_gain_ref, q_grad_ref), (k_ref, k_gain_ref, k_grad_ref))
            for part, (raw_ref, gain_ref, out_ref) in enumerate(refs):
                grad = packed_ref[micro * heads + head, :, part * size : (part + 1) * size]
                grad = grad.astype(f32)
                grad = grad * cos_ref[...] + turn_back(grad * sin_ref[...])
                out_ref[here, lanes] = grad
                product = grad * raw_ref[here, lanes]
                sums[part] = sums[part] + jnp.sum(
                    product * gain_ref[:, lanes], axis=1, keepdims=True
                )
                gains_ref[part : part + 1, lanes] += jnp.sum(
                    product * scales_ref[here, part : part + 1], axis=0, keepdims=True
                )
            v_grad_ref[here, lanes] = packed_ref[micro * heads + head, :, 2 * size :]
        dots.append(in_lanes(*sums))
    dots_ref[...] = as_row(jnp.concatenate(dots, axis=0))


def unturn(packed, query, key, gains, cosine, sine, scales):
    count, local_width = query.shape
    raw = jax.ShapeDtypeStruct((count, local_width), f32)
    return pl.pallas_call(
        unturn_kernel,
        out_shape=[
            raw,
            raw,
            jax.ShapeDtypeStruct((count, local_width), bf16),
            jax.ShapeDtypeStruct((8, count), f32),
            jax.ShapeDtypeStruct((8, local_width), f32),
        ],
        in_specs=in_vmem(8),
        out_specs=in_vmem(5),
        compiler_params=kernel_params(),
    )(packed, query, key, *gains, cosine, sine, scales)


def norm_back_kernel(
    own_rows, width, partners, q_grad_ref, k_grad_ref, q_ref, k_ref, q_gain_ref, k_gain_ref, scales_ref, own_ref, *refs
):
    outs = refs[partners:]
    dots = summed_rows(own_ref, refs[:partners], own_rows)
    refs = ((q_grad_ref, q_ref, q_gain_ref), (k_grad_ref, k_ref, k_gain_ref))
    for part, (grad_ref, raw_ref, gain_ref) in enumerate(refs):
        scale = scales_ref[:, part : part + 1]
        dot = dots[:, part : part + 1]
        grad = scale * gain_ref[...] * grad_ref[...] - raw_ref[...] * (scale**3 * dot / width)
        outs[part][...] = grad.astype(bf16)


def norm_back(q_grad, k_grad, query, key, gains, scales, dots, arrived, own_rows, width):
    count, local_width = query.shape
    return pl.pallas_call(
        functools.partial(norm_back_kernel, own_rows, width, len(arrived)),
        out_shape=[jax.ShapeDtypeStruct((count, local_width), bf16)] * 2,
        in_specs=in_vmem(8 + len(arrived)),
        out_specs=in_vmem(2),
        compiler_params=kernel_params(),
    )(q_grad, k_grad, query, key, *gains, scales, dots, *arrived)


def project_back_kernel(
    q_ref, k_ref, v_ref, rows_ref, scale_ref, query_ref, key_ref, value_ref, out_ref, gain_ref
):
    part = (
        mm_t(q_ref[...], query_ref[...])
        + mm_t(k_ref[...], key_ref[...])
        + mm_t(v_ref[...], value_ref[...])
    )
    out_ref[...] = part.astype(bf16)
    rows = rows_ref[...].astype(f32) * scale_ref[...]
    gain_ref[...] = jnp.sum(part * rows, axis=0, keepdims=True)


def project_back(query_grad, key_grad, value_grad, rows, scale, w_query, w_key, w_value):
    count, width = rows.shape
    local_width = w_query.shape[1]
    block = min(512, width)
    whole = lambda *shape: pl.BlockSpec(shape, lambda step: (0, 0))
    weight = pl.BlockSpec((block, local_width), lambda step: (step, 0))
    cut = pl.BlockSpec((count, block), lambda step: (0, step))
    return pl.pallas_call(
        project_back_kernel,
        grid=(width // block,),
        out_shape=[
            jax.ShapeDtypeStruct((count, width), bf16),
            jax.ShapeDtypeStruct((1, width), f32),
        ],
        in_specs=[
            whole(count, local_width),
            whole(count, local_width),
            whole(count, local_width),
            cut,
            whole(count, 1),
            weight,
            weight,
            weight,
        ],
        out_specs=[cut, pl.BlockSpec((1, block), lambda step: (0, step))],
        compiler_params=kernel_params(),
    )(query_grad, key_grad, value_grad, rows, scale, w_query, w_key, w_value)


def rows_back_kernel(
    parts_ref, residual_ref, normed_ref, mask_ref, router_ref, gain_ref, upstream_ref,
    grad_ref, low_ref, router_grad_ref, gain_grad_ref,
):
    width = residual_ref.shape[1]
    experts = router_ref.shape[1]
    total = parts_ref[0].astype(f32)
    for number in range(1, parts_ref.shape[0]):
        total = total + parts_ref[number].astype(f32)
    normed = normed_ref[...]
    logits = mm(normed, router_ref[...])
    probs = jnp.exp(logits - jnp.max(logits, axis=1, keepdims=True))
    probs = probs / jnp.sum(probs, axis=1, keepdims=True)
    prob_grad = total[:, width : width + experts] * mask_ref[:, :experts].astype(f32)
    logit_grad = probs * (prob_grad - jnp.sum(prob_grad * probs, axis=1, keepdims=True))
    logit_grad = logit_grad.astype(bf16)
    grad = total[:, :width] + mm_t(logit_grad, router_ref[...])
    router_grad_ref[...] = t_mm(logit_grad, normed)
    residual = residual_ref[...]
    scale = rms_scale(residual)
    scaled = residual * scale
    gain_grad_ref[...] = jnp.sum(grad * scaled, axis=0, keepdims=True)
    weighted = grad * gain_ref[...]
    back = (
        upstream_ref[...].astype(f32)
        + scale * weighted
        - scaled * (scale**2 * jnp.mean(weighted * residual, axis=1, keepdims=True))
    )
    grad_ref[...] = back
    low_ref[...] = back.astype(bf16)


def rows_back(parts, residual, normed, mask, router, gain, upstream):
    rows, width = residual.shape
    return pl.pallas_call(
        rows_back_kernel,
        out_shape=[
            jax.ShapeDtypeStruct((rows, width), f32),
            jax.ShapeDtypeStruct((rows, width), bf16),
            jax.ShapeDtypeStruct((router.shape[1], width), f32),
            jax.ShapeDtypeStruct((1, width), f32),
        ],
        in_specs=in_vmem(7),
        out_specs=in_vmem(4),
        compiler_params=kernel_params(),
    )(parts, residual, normed, mask, router, gain[None], upstream)


def attention_forward(query, key, value, causal, scale):
    scores = mm_t(query, key) * scale
    scores = jnp.where(causal, scores, masked_score)
    highest = jnp.max(scores, axis=1, keepdims=True)
    log_total = highest + jnp.log(jnp.sum(jnp.exp(scores - highest), axis=1, keepdims=True))
    probs_low = jnp.exp(scores - log_total).astype(bf16)
    return mm(probs_low, value).astype(bf16), log_total


def attention_backward(query, key, value, log_total, grad, causal, scale):
    scores = mm_t(query, key) * scale
    scores = jnp.where(causal, scores, masked_score)
    probs = jnp.exp(scores - log_total)
    probs_low = probs.astype(bf16)
    dprob = mm_t(grad, value)
    score_grad = (probs * (dprob - jnp.sum(dprob * probs, axis=1, keepdims=True))).astype(bf16)
    return (
        (mm(score_grad, key) * scale).astype(bf16),
        (t_mm(score_grad, query) * scale).astype(bf16),
        t_mm(probs_low, grad).astype(bf16),
    )


def shards(
    tokens,
    out_grad,
    routes,
    norm1_gain,
    w_query,
    w_key,
    w_value,
    query_gain,
    key_gain,
    w_output,
    norm2_gain,
    w_router,
    w_gate,
    w_up,
    w_down,
):
    micro_count, rows_here, width = tokens.shape
    local_width = w_query.shape[1]
    heads_here, head_size = query_gain.shape
    experts = w_router.shape[1]
    groups = lax.axis_size("expert")
    tensor_count = lax.axis_size("tensor")
    owned, _, hidden_width = w_gate.shape
    own_rows = rows_here // tensor_count
    flat_rows = micro_count * rows_here
    score_scale = head_size ** (-0.5)
    expert_at = lax.axis_index("expert")
    tensor_at = lax.axis_index("tensor")

    expert_bits = bits_of(groups)
    tensor_bits = bits_of(tensor_count)
    tensor_steps = [("tensor", bit) for bit in tensor_bits]
    tensor_order = partner_order(tensor_bits)

    def by_partner(operand):
        return jnp.concatenate(
            [
                lax.dynamic_slice_in_dim(operand, (tensor_at ^ place) * own_rows, own_rows, axis=1)
                for place in tensor_order
            ],
            axis=1,
        )

    def in_sequence(operand):
        place_of = jnp.asarray(
            [tensor_order.index(place) for place in range(tensor_count)], jnp.int32
        )
        return jnp.concatenate(
            [
                lax.dynamic_slice_in_dim(
                    operand, place_of[tensor_at ^ place] * own_rows, own_rows, axis=1
                )
                for place in range(tensor_count)
            ],
            axis=1,
        )

    pairs = micro_count * heads_here
    per_device = max(1, pairs // groups)
    copies = max(1, groups // pairs)

    def to_heads(operand, work=None):
        wide = operand.shape[3]
        return pairs_to_heads(
            operand.transpose(0, 2, 1, 3).reshape(pairs, rows_here, wide), work
        )

    def pairs_to_heads(blocks, work=None):
        wide = blocks.shape[2]
        if copies > 1:
            blocks = jnp.repeat(blocks, copies, axis=0)
        arrived = lax.all_to_all(blocks, "expert", split_axis=0, concat_axis=0, tiled=True)
        if work is not None:
            arrived = after(arrived, *work(blocks))
        blocks = arrived.reshape(groups, per_device, rows_here, wide)
        return blocks.transpose(1, 0, 2, 3).reshape(per_device, groups * rows_here, wide)

    def pairs_from_heads(operand, others=()):
        wide = operand.shape[2]
        blocks = operand.reshape(per_device, groups, rows_here, wide).transpose(1, 0, 2, 3)
        blocks = blocks.reshape(groups * per_device, rows_here, wide)
        blocks = lax.all_to_all(blocks, "expert", split_axis=0, concat_axis=0, tiled=True)
        if others:
            blocks = after(blocks, *others)
        if copies > 1:
            blocks = blocks[::copies]
        return blocks

    def from_heads(operand, others=()):
        blocks = pairs_from_heads(operand, others)
        wide = blocks.shape[2]
        return blocks.reshape(micro_count, heads_here, rows_here, wide).transpose(0, 2, 1, 3)

    row_number = jnp.arange(own_rows, dtype=jnp.int32)
    row_in_block = jnp.concatenate(
        [(tensor_at ^ place) * own_rows + row_number for place in tensor_order]
    )
    row_pos = expert_at * rows_here + row_in_block
    frequency = theta_base ** (-(jnp.arange(head_size // 2, dtype=f32) * 2.0 / head_size))
    angles = row_pos.astype(f32)[:, None] * frequency[None, :]
    angles = jnp.concatenate([angles, angles], axis=1)
    cosine = jnp.cos(angles)
    sine = jnp.sin(angles)
    sequence_pos = (
        jnp.arange(groups, dtype=jnp.int32)[:, None] * rows_here + row_in_block[None, :]
    ).reshape(-1)
    causal = sequence_pos[None, :] <= sequence_pos[:, None]

    near, side = 1, tensor_bits[0]
    far = groups // 2
    far_groups = [[2 * place + last for place in range(far)] for last in range(2)]
    copy_count = tensor_count // 2

    def far_exchange(blocks):
        return lax.all_to_all(
            blocks, "expert", split_axis=0, concat_axis=0, axis_index_groups=far_groups, tiled=True
        )

    def gather_far(rows, work=None):
        block = far_exchange(jnp.broadcast_to(rows[None], (far,) + rows.shape))
        if work is not None:
            block = after(block, *work())
        return block.reshape((far * rows.shape[0],) + rows.shape[1:])

    def gather_sides(block, work=None):
        arrived = [swap(block, "expert", near), swap(block, "tensor", side)]
        return after_all(arrived, *work()) if work is not None else arrived

    def gather_diagonal(by_near, by_side):
        half = by_near.shape[0] // 2
        low, high = swap(by_side[:half], "expert", near), swap(by_near[half:], "tensor", side)
        return jnp.concatenate([low, high], axis=0)

    def gather_rest(block, by_near, by_side):
        half = block.shape[0] // 2
        by_both_low = swap(by_side[:half], "expert", near)
        by_both_high = swap(by_near[half:], "tensor", side)
        copies = [[[block, by_near], [by_side, by_both_low, by_both_high]]]
        for bit in tensor_bits[1:]:
            copies = copies + [
                [[swap(piece, "tensor", bit) for piece in call] for call in copy]
                for copy in copies
            ]
        return [[copy[call] for copy in copies] for call in range(2)]

    def add(*terms):
        total = terms[0].astype(f32)
        for term in terms[1:]:
            total = total + term.astype(f32)
        return total

    def reduce_copies(parts, work=None):
        for bit in tensor_bits[1:][::-1]:
            half = len(parts) // 2
            arrived = [swap(part, "tensor", bit) for part in parts[half:]]
            if work is not None and half == 1:
                arrived = after_all(arrived, *work(parts[1]))
            parts = [add(part, other).astype(bf16) for part, other in zip(parts[:half], arrived)]
        return parts[0]

    def reduce_diagonal(second, work=None):
        half, quarter = second.shape[0] // 2, second.shape[0] // 4
        low, high = second[half : half + quarter], second[half + quarter :]
        arrived = [swap(low, "expert", near), swap(high, "tensor", side)]
        return after_all(arrived, *work(low)) if work is not None else arrived

    def side_parts(first, second, from_near, from_side):
        half, quarter = second.shape[0] // 2, second.shape[0] // 4
        near_part = [first[half : half + quarter], add(first[half + quarter :], from_side)]
        side_part = [add(second[:quarter], from_near), second[quarter:half]]
        return [
            jnp.concatenate([part.astype(bf16) for part in parts], axis=0)
            for parts in (near_part, side_part)
        ]

    def reduce_sides(near_part, side_part, work=None):
        arrived = [swap(near_part, "expert", near), swap(side_part, "tensor", side)]
        return after_all(arrived, *work(near_part)) if work is not None else arrived

    def far_block(first, by_near, by_side):
        return add(first[: first.shape[0] // 2], by_near, by_side).astype(bf16)

    def reduce_far(block, work=None):
        parts = far_exchange(block.reshape((far, block.shape[0] // far) + block.shape[1:]))
        if work is not None:
            parts = after(parts, *work(block))
        return parts

    def far_sum(parts):
        return jnp.sum(parts.astype(f32), axis=0)

    high_bits = [bit for bit in expert_bits if bit >= 4]
    low_places = [place for place in range(1, min(4, groups))]

    def columns_of(operand, low_place):
        block = operand.shape[1] // groups
        return jnp.concatenate(
            [
                lax.dynamic_slice_in_dim(
                    operand, (expert_at ^ low_place ^ place) * block, block, axis=1
                )
                for place in partner_order(high_bits)
            ],
            axis=1,
        )

    near_count = min(4, groups)
    near_groups = [
        [first + place for place in range(near_count)] for first in range(0, groups, near_count)
    ]

    def near_exchange(operand):
        block = operand.shape[1] // groups
        high = expert_at - expert_at % near_count
        parts = [
            jnp.concatenate(
                [
                    lax.dynamic_slice_in_dim(
                        operand, ((high ^ above) + place) * block, block, axis=1
                    )
                    for above in partner_order(high_bits)
                ],
                axis=1,
            )
            for place in range(near_count)
        ]
        arrived = lax.all_to_all(
            jnp.stack(parts),
            "expert",
            split_axis=0,
            concat_axis=0,
            axis_index_groups=near_groups,
            tiled=True,
        )
        return arrived.reshape(near_count * flat_rows, -1)

    def near_gather(operand):
        return lax.all_gather(
            operand, "expert", axis_index_groups=near_groups, axis=0, tiled=True
        )

    def near_rows(gathered, place):
        return lax.dynamic_slice_in_dim(
            gathered, ((expert_at % 4) ^ place) * flat_rows, flat_rows, axis=0
        )

    def near_swaps(operand):
        return [swap(operand, "expert", place) for place in low_places]

    def halve_product(product):
        return halve_rows(product, [("expert", bit) for bit in high_bits[::-1]], 0, f32)

    grad_rows = lax.dynamic_slice_in_dim(out_grad, tensor_at * own_rows, own_rows, axis=1)
    route_rows = lax.dynamic_slice_in_dim(routes, tensor_at * own_rows, own_rows, axis=1)
    mask_rows = jnp.sum(
        (route_rows[..., None] == jnp.arange(experts, dtype=jnp.int32)).astype(f32), axis=2
    )
    upstream = jnp.concatenate(
        [grad_rows, jnp.pad(mask_rows, ((0, 0), (0, 0), (0, 128 - experts))).astype(bf16)], axis=2
    )
    upstream = upstream.reshape(micro_count * own_rows, width + 128)
    upstream_gathered = lax.all_gather(upstream, ("expert", "tensor"), axis=0, tiled=True)

    tokens_here = by_partner(tokens)
    flat_tokens = tokens_here.reshape(flat_rows, width)
    norm_in, query_raw, key_raw, value_low, squares = project(
        flat_tokens, norm1_gain, w_query, w_key, w_value
    )
    gains = [query_gain.reshape(1, local_width), key_gain.reshape(1, local_width)]
    head_shape = (micro_count, rows_here, heads_here, head_size)

    def from_partners(operand):
        return [swap(operand, "tensor", place) for place in tensor_order[1:]]

    packed, scales = turn_and_pack(
        query_raw,
        key_raw,
        value_low,
        gains,
        cosine,
        sine,
        squares,
        from_partners(squares),
        own_rows,
        width,
        pairs,
    )
    packed = pairs_to_heads(packed)
    head_parts = []
    for number in range(per_device):
        parts = [
            packed[number, :, part * head_size : (part + 1) * head_size] for part in range(3)
        ]
        head_parts.append((parts, attention_forward(*parts, causal, score_scale)))
    attended = from_heads(jnp.stack([out for _, (out, _) in head_parts]))
    attended = attended.reshape(flat_rows, local_width)

    attn_part = mm(attended, w_output).astype(bf16).reshape(micro_count, rows_here, width)
    halves = jnp.split(attn_part, 2, axis=1)
    attn_half = add(halves[0], swap(halves[1], *tensor_steps[-1]))
    attn_rows = halve_rows(attn_half.astype(bf16), tensor_steps[:-1][::-1], 1, f32)
    own_source = tokens_here[:, :own_rows].astype(f32)
    residual = (own_source + attn_rows).reshape(micro_count * own_rows, width)
    norm_out = (residual * rms_scale(residual) * norm2_gain).astype(bf16)

    expert_base = jnp.reshape(expert_at * owned, (1,)).astype(jnp.int32)
    table = []
    for call in range(2):
        for copy_place in partner_order(tensor_bits[1:]):
            for last in range(2):
                for place in range(far):
                    owner = 2 * place + (expert_at % 2 ^ last)
                    table.append(
                        owner * tensor_count + (tensor_at ^ (copy_place ^ (call * side)))
                    )
    table = jnp.stack(table).astype(jnp.int32)
    upstream_made = []

    def upstream_work(call, token):
        def work():
            upstream_made.append(
                upstream_products(
                    call,
                    2,
                    table,
                    upstream_gathered,
                    w_down,
                    [upstream_made[-1][2]] if upstream_made else [],
                    [token],
                )
            )
            return upstream_made[-1][:1]

        return work

    block = gather_far(norm_out, upstream_work(0, norm_out))
    by_near, by_side = gather_sides(block, upstream_work(1, block))
    gathered = gather_rest(block, by_near, by_side)
    upstream_all = upstream_made[-1][2]
    total_rows = micro_count * groups * rows_here
    kept = []

    def expert_rows(call):
        nonlocal kept
        copies = gathered[call]
        rows = sum(piece.shape[0] for piece in copies[0])
        count = min(copy_count, max(1, expert_rows_most // rows))
        all_parts = []
        for part in range(copy_count // count):
            parts, kept = expert_call(
                call * (copy_count // count) + part,
                total_rows,
                part,
                expert_base,
                copies[part * count : (part + 1) * count],
                rows // 2,
                upstream_made[call][1],
                w_router,
                w_gate,
                w_up,
                upstream_made[call][0],
                kept,
            )
            all_parts += parts
        return all_parts

    made = {}

    def down_work(call):
        def work(token):
            made[call] = down_products(call, 2, copy_count, kept[1], w_down, [token])
            return list(made[call][:1])

        return work

    def grad_work(name, left, right, *others):
        def work(token):
            tokens = token if isinstance(token, list) else [token]
            made[name] = expert_grads(left, right, owned, tokens)
            return [made[name], *others]

        return work

    attended_gathered = near_gather(after(attended, gathered[1][0][-1]))
    first = expert_rows(0)
    norm_in_gathered = near_exchange(after(norm_in, first[0]))
    first = reduce_copies(first)
    second = expert_rows(1)
    second = reduce_copies([after(second[0], norm_in_gathered)] + second[1:])
    near_part, side_part = side_parts(first, second, *reduce_diagonal(second, down_work(0)))
    arrived = reduce_sides(
        near_part,
        side_part,
        lambda token: down_work(1)(token) + grad_work("down", kept[1], upstream_all)(token),
    )
    out_first, out_second = (reduce_copies(made[call]) for call in range(2))
    out_diagonal = reduce_diagonal(out_second)
    row_parts = reduce_far(
        far_block(first, *arrived),
        lambda token: grad_work("gate", kept[0], kept[2])([token, out_first, out_second]),
    )
    residual_grad, residual_low, router_part, second_gain_part = rows_back(
        row_parts,
        residual,
        norm_out,
        upstream[:, width:],
        w_router,
        norm2_gain,
        grad_rows.reshape(micro_count * own_rows, width),
    )
    out_sides = reduce_sides(
        *side_parts(out_first, out_second, *after_all(out_diagonal, residual_low))
    )
    residual_grad, residual_low = (
        item.reshape(micro_count, own_rows, width) for item in (residual_grad, residual_low)
    )
    residual_low = jnp.concatenate(
        [residual_low, swap(residual_low, *tensor_steps[0])], axis=1
    )
    residual_low = double_rows(residual_low, tensor_steps[1:], 1).reshape(flat_rows, width)

    attended_grad = mm_t(residual_low, w_output).astype(bf16).reshape(head_shape)
    attended_grad = to_heads(attended_grad, grad_work("up", kept[0], kept[3], *out_sides))
    head_grads = []
    for number in range(per_device):
        parts, (_, log_total) = head_parts[number]
        grads = attention_backward(*parts, log_total, attended_grad[number], causal, score_scale)
        head_grads.append(jnp.concatenate(grads, axis=1))
    residual_gathered = near_exchange(after(residual_low, attended_grad))
    head_grads = after(jnp.stack(head_grads), residual_gathered)
    out_block = far_block(out_first, *after_all(out_sides, attended_grad))
    packed_grad = pairs_from_heads(head_grads)
    out_parts = reduce_far(after(out_block, packed_grad))
    normed_q_grad, normed_k_grad, value_grad_low, row_dots, gain_parts = unturn(
        packed_grad, query_raw, key_raw, gains, cosine, sine, scales
    )
    value_arrived = near_swaps(value_grad_low)
    query_grad_low, key_grad_low = norm_back(
        normed_q_grad,
        normed_k_grad,
        query_raw,
        key_raw,
        gains,
        scales,
        row_dots,
        [after(dots, out_parts) for dots in from_partners(row_dots)],
        own_rows,
        width,
    )
    query_arrived = near_swaps(query_grad_low)
    norm_in_there = after(norm_in_gathered, query_grad_low)
    norm_in_near = jnp.concatenate(
        [near_rows(norm_in_there, place) for place in range(near_count)], axis=0
    )

    def near_product(own, arrived, *others):
        right = jnp.concatenate([own] + after_all(arrived, *others), axis=0)
        return t_mm(norm_in_near, right).astype(bf16)

    value_product = near_product(value_grad_low, value_arrived, query_grad_low)
    query_arrived = after_all(query_arrived, value_product)
    key_arrived = near_swaps(after(key_grad_low, *query_arrived))
    query_product = near_product(query_grad_low, query_arrived)
    key_arrived = after_all(key_arrived, query_product)
    key_product = near_product(key_grad_low, key_arrived)
    grad_value, grad_query = (halve_product(item) for item in (value_product, query_product))
    grad_key = halve_product(key_product)
    output_product = t_mm(residual_gathered, after(attended_gathered, query_grad_low))
    grad_output = halve_product(output_product.astype(bf16)).T
    out_rows = far_sum(after(out_parts, query_product))
    layer_out = (residual + out_rows).astype(bf16)
    layer_out = layer_out.reshape(micro_count, own_rows, tensor_count, -1).transpose(2, 0, 1, 3)
    layer_out = lax.all_to_all(layer_out, "tensor", split_axis=0, concat_axis=0, tiled=True)
    layer_out = layer_out.transpose(1, 0, 2, 3).reshape(micro_count, rows_here, -1)

    column_block = width // groups

    def reduce_small(rows):
        rows = jnp.pad(rows, ((0, -rows.shape[0] % 16), (0, 0))).astype(bf16)
        rows = rows.reshape(-1, groups, column_block).transpose(1, 0, 2)
        rows = lax.all_to_all(rows, "expert", split_axis=0, concat_axis=0, tiled=True)
        rows = jnp.sum(rows.astype(f32), axis=0).astype(bf16)
        return sum_over(rows, tensor_steps).astype(f32)

    head_block = head_size // groups
    head_gains = gain_parts[:2].reshape(2 * heads_here, groups, head_block)
    head_gains = head_gains.transpose(1, 0, 2).reshape(groups, 2 * heads_here * head_block)
    head_gains = jnp.pad(head_gains, ((0, 0), (0, column_block - head_gains.shape[1])))
    head_rows = jnp.where(
        jnp.arange(tensor_count, dtype=jnp.int32)[:, None] == tensor_at,
        head_gains.reshape(1, width),
        0.0,
    )
    small = reduce_small(
        after(jnp.concatenate([router_part, second_gain_part, head_rows], axis=0), query_product)
    )
    grad_router = small[:experts].T
    own_heads = lax.dynamic_slice_in_dim(small, experts + 1 + tensor_at, 1, axis=0)
    own_heads = own_heads[0, : 2 * heads_here * head_block].reshape(2, heads_here, head_block)

    scale_in = rms_scale(tokens_here.astype(f32))
    norm_in_part, first_gain_part = project_back(
        after(query_grad_low, query_product),
        key_grad_low,
        value_grad_low,
        flat_tokens,
        scale_in.reshape(flat_rows, 1),
        w_query,
        w_key,
        w_value,
    )
    norm_in_grad = halve_rows(
        norm_in_part.reshape(micro_count, rows_here, width),
        tensor_steps[::-1],
        1,
        f32,
    )
    own_scale = scale_in[:, :own_rows]
    weighted_in = norm_in_grad * norm1_gain
    tokens_grad = (
        residual_grad
        + own_scale * weighted_in
        - own_source * own_scale**3 * jnp.mean(weighted_in * own_source, axis=2, keepdims=True)
    )
    tokens_grad = in_sequence(double_rows(tokens_grad.astype(bf16), tensor_steps, 1)).astype(f32)

    first_gain = reduce_small(first_gain_part)
    return (
        layer_out,
        tokens_grad,
        first_gain[0],
        grad_query,
        grad_key,
        grad_value,
        own_heads[0],
        own_heads[1],
        grad_output,
        small[experts],
        grad_router,
        made["gate"],
        made["up"],
        made["down"],
    )


def solution(mesh):
    placed = (
        P(None, "expert", None),
        P(None, "expert", None),
        P(None, "expert", None),
        P(),
        P(None, "tensor"),
        P(None, "tensor"),
        P(None, "tensor"),
        P("tensor", None),
        P("tensor", None),
        P("tensor", None),
        P(),
        P(),
        P("expert", None, "tensor"),
        P("expert", None, "tensor"),
        P("expert", "tensor", None),
    )
    return jax.shard_map(
        shards,
        mesh=mesh,
        in_specs=placed,
        out_specs=(
            P(None, "expert", "tensor"),
            P(None, "expert", None),
            P("expert"),
            P("expert", "tensor"),
            P("expert", "tensor"),
            P("expert", "tensor"),
            P("tensor", "expert"),
            P("tensor", "expert"),
            P("tensor", "expert"),
            P("expert"),
            P("expert", None),
            P("expert", None, "tensor"),
            P("expert", None, "tensor"),
            P("expert", "tensor", None),
        ),
        check_vma=False,
    )
```

```python
import functools

import jax
import jax.numpy as jnp
from jax import lax
from jax.experimental import pallas as pl
from jax.experimental.pallas import tpu as pltpu
from jax.sharding import PartitionSpec as P

eps = 1e-05
theta_base = 10000.0
masked_score = -1e30
bf16 = jnp.bfloat16
f32 = jnp.float32
vmem_limit = 56 * 1024 * 1024
expert_rows_most = 1024


def rms_scale(operand):
    return lax.rsqrt(jnp.mean(operand * operand, axis=-1, keepdims=True) + eps)


def turn_half(operand):
    middle = operand.shape[-1] // 2
    return jnp.concatenate([-operand[..., middle:], operand[..., :middle]], axis=-1)


def turn_back(operand):
    middle = operand.shape[-1] // 2
    return jnp.concatenate([operand[..., middle:], -operand[..., :middle]], axis=-1)


def bits_of(count):
    bits = []
    bit = count // 2
    while bit:
        bits.append(bit)
        bit //= 2
    return bits


def partner_order(bits):
    order = [0]
    for bit in bits:
        order = order + [place ^ bit for place in order]
    return order


def swap(operand, axis_name, bit):
    count = lax.axis_size(axis_name)
    return lax.ppermute(operand, axis_name, [(i, i ^ bit) for i in range(count)])


def double_rows(operand, steps, axis):
    for axis_name, bit in steps:
        operand = jnp.concatenate([operand, swap(operand, axis_name, bit)], axis=axis)
    return operand


def halve_rows(operand, steps, axis, last=bf16):
    for number, (axis_name, bit) in enumerate(steps):
        half = operand.shape[axis] // 2
        kept = lax.slice_in_dim(operand, 0, half, axis=axis)
        sent = lax.slice_in_dim(operand, half, 2 * half, axis=axis)
        total = kept.astype(f32) + swap(sent, axis_name, bit).astype(f32)
        operand = total if number == len(steps) - 1 and last == f32 else total.astype(bf16)
    return operand


def sum_over(operand, steps):
    for axis_name, bit in steps:
        operand = operand + swap(operand, axis_name, bit)
    return operand


def sum_over_rows(operand, steps, own_rows):
    shape = operand.shape
    blocked = operand.reshape((-1,) + (2,) * len(steps) + (own_rows,))
    for number, (axis_name, bit) in enumerate(steps):
        blocked = blocked + jnp.flip(swap(blocked, axis_name, bit), axis=len(steps) - number)
    return blocked.reshape(shape)


def mm(left, right):
    return jnp.dot(left, right, preferred_element_type=f32)


def mm_t(left, right):
    return lax.dot_general(left, right, (((1,), (1,)), ((), ())), preferred_element_type=f32)


def t_mm(left, right):
    return lax.dot_general(left, right, (((0,), (0,)), ((), ())), preferred_element_type=f32)


def after(operand, *others):
    def nothing(*refs):
        pass

    anywhere = pl.BlockSpec(memory_space=pl.ANY)
    return pl.pallas_call(
        nothing,
        out_shape=jax.ShapeDtypeStruct(operand.shape, operand.dtype),
        in_specs=[anywhere] * (1 + len(others)),
        out_specs=anywhere,
        input_output_aliases={0: 0},
    )(operand, *others)


def after_all(operands, *others):
    return [after(operand, *others) for operand in operands] if others else list(operands)


def upstream_kernel(place, blocks, width, table_ref, down_ref, gathered_ref, *refs):
    back_ref, mask_ref, rows_ref, sems = refs[-4:]
    own_rows = rows_ref.shape[0] // blocks

    @pl.when(pl.program_id(0) == 0)
    def _():
        copies = []
        for number in range(blocks):
            start = pl.multiple_of(table_ref[place * blocks + number] * own_rows, own_rows)
            source = gathered_ref.at[pl.ds(start, own_rows)]
            there = pl.ds(number * own_rows, own_rows)
            copies.append(
                pltpu.make_async_copy(
                    source.at[:, pl.ds(0, width)], rows_ref.at[there], sems.at[0, number]
                )
            )
            copies.append(
                pltpu.make_async_copy(
                    source.at[:, pl.ds(width, 128)], mask_ref.at[there], sems.at[1, number]
                )
            )
        for copy in copies:
            copy.start()
        for copy in copies:
            copy.wait()

    back_ref[...] = mm_t(rows_ref[...], down_ref[0])


def upstream_products(place, calls, table, gathered, w_down, kept, tokens):
    owned, hidden_width, width = w_down.shape
    blocks = table.shape[0] // calls
    rows = gathered.shape[0] // calls
    anywhere = pl.BlockSpec(memory_space=pl.ANY)
    others = [gathered] + kept + tokens
    return pl.pallas_call(
        functools.partial(upstream_kernel, place, blocks, width),
        out_shape=[
            jax.ShapeDtypeStruct((rows, owned * hidden_width), f32),
            jax.ShapeDtypeStruct((rows, 128), bf16),
            jax.ShapeDtypeStruct((calls * rows, width), bf16),
        ],
        grid_spec=pltpu.PrefetchScalarGridSpec(
            num_scalar_prefetch=1,
            grid=(owned,),
            in_specs=[pl.BlockSpec((1, hidden_width, width), lambda step, table: (step, 0, 0))]
            + [anywhere] * len(others),
            out_specs=[
                pl.BlockSpec((rows, hidden_width), lambda step, table: (0, step)),
                pl.BlockSpec((rows, 128), lambda step, table: (0, 0)),
                pl.BlockSpec((rows, width), lambda step, table: (place, 0)),
            ],
            scratch_shapes=[pltpu.SemaphoreType.DMA((2, blocks))],
        ),
        input_output_aliases={3: 2} if kept else {},
        compiler_params=pltpu.CompilerParams(vmem_limit_bytes=vmem_limit),
        cost_estimate=pl.CostEstimate(
            flops=2 * rows * width * owned * hidden_width,
            bytes_accessed=8 * rows * width,
            transcendentals=0,
        ),
    )(table, w_down, *others)


def expert_kernel(
    plan, copy_count, width, base_ref, mask_ref, router_ref, gate_ref, up_ref, back_ref, *refs
):
    piece_count = sum(len(block) for block in plan)
    piece_refs = refs[:piece_count]
    part_refs = refs[-11 - copy_count : -11]
    copy_ref, gated_ref, gate_back_ref, up_back_ref = refs[-11:-7]
    rows, gates, ups, probs, row_sems, gate_sems, up_sems = refs[-7:]
    step = pl.program_id(0)
    experts = router_ref.shape[1]
    owned, _, hidden_width = gate_ref.shape

    def row_copies(block):
        copies, start = [], 0
        first = sum(len(item) for item in plan[:block])
        for number in range(len(plan[block])):
            piece_ref = piece_refs[first + number]
            count = piece_ref.shape[0]
            copies.append(
                pltpu.make_async_copy(
                    piece_ref,
                    rows.at[block % 2, pl.ds(start, count)],
                    row_sems.at[block % 2, number],
                )
            )
            start += count
        return copies

    def weight_copies(number):
        here = pl.ds(number * hidden_width, hidden_width)
        return [
            pltpu.make_async_copy(gate_ref.at[number], gates.at[:, here], gate_sems.at[number]),
            pltpu.make_async_copy(up_ref.at[number], ups.at[:, here], up_sems.at[number]),
        ]

    @pl.when(step == 0)
    def _():
        for copy in row_copies(0):
            copy.start()
        for number in range(owned):
            for copy in weight_copies(number):
                copy.start()

    for block in range(len(plan)):

        @pl.when(step == block)
        def _(block=block):
            for copy in row_copies(block):
                copy.wait()
            if block + 1 < len(plan):
                for copy in row_copies(block + 1):
                    copy.start()

    own_rows = rows[step % 2]
    copy_ref[...] = own_rows
    logits = mm(own_rows, router_ref[...])
    weights = jnp.exp(logits - jnp.max(logits, axis=1, keepdims=True))
    weights = weights / jnp.sum(weights, axis=1, keepdims=True)
    probs[...] = weights * mask_ref[:, :experts].astype(f32)
    lane = lax.broadcasted_iota(jnp.int32, probs.shape, 1)
    slope_lane = lax.broadcasted_iota(jnp.int32, (own_rows.shape[0], 128), 1)

    slopes = jnp.zeros(slope_lane.shape, f32)
    for number in range(owned):
        here = slice(number * hidden_width, (number + 1) * hidden_width)
        owner = base_ref[0] + number

        @pl.when(step == 0)
        def _(number=number):
            for copy in weight_copies(number):
                copy.wait()

        gate = jnp.sum(jnp.where(lane == owner, probs[...], 0.0), axis=1, keepdims=True)
        gate_pre = mm(rows[step % 2], gates[:, here])
        up_pre = mm(rows[step % 2], ups[:, here])
        back = back_ref[:, here]
        sigmoid_gate = 1.0 / (1.0 + jnp.exp(-gate_pre))
        activated = gate_pre * sigmoid_gate
        hidden = activated * up_pre
        gated_ref[:, here] = (gate * hidden).astype(bf16)
        slope = jnp.sum(hidden * back, axis=1, keepdims=True)
        slopes = slopes + jnp.where(slope_lane == owner, slope, 0.0)
        hidden_grad = gate * back
        gate_back_ref[:, here] = (
            hidden_grad * up_pre * (sigmoid_gate * (1.0 + gate_pre * (1.0 - sigmoid_gate)))
        ).astype(bf16)
        up_back_ref[:, here] = (hidden_grad * activated).astype(bf16)
    part = mm_t(gate_back_ref[...], gates[...]) + mm_t(up_back_ref[...], ups[...])
    part = part.astype(bf16)
    per_copy = len(plan) // copy_count
    for copy, part_ref in enumerate(part_refs):

        @pl.when(step // per_copy == copy)
        def _(part_ref=part_ref):
            part_ref[:, :width] = part
            part_ref[:, width:] = slopes.astype(bf16)


def expert_call(
    place, total_rows, part, base, copies, block_rows, mask, router, w_gate, w_up, back, kept
):
    plan, pieces = [], []
    for copy in copies:
        for piece in copy:
            if not plan or sum(item.shape[0] for item in plan[-1]) == block_rows:
                plan.append([])
            plan[-1].append(piece)
            pieces.append(piece)
    copy_count = len(copies)
    per_copy = len(plan) // copy_count
    owned, width, hidden_width = w_gate.shape
    hidden = owned * hidden_width
    experts = router.shape[1]
    blocks = len(plan)
    anywhere = pl.BlockSpec(memory_space=pl.ANY)
    here = lambda step, base_ref: (place * blocks + step, 0)
    in_specs = [
        pl.BlockSpec((block_rows, 128), lambda step, base_ref: (part * blocks + step, 0)),
        pl.BlockSpec((width, experts), lambda step, base_ref: (0, 0)),
        anywhere,
        anywhere,
        pl.BlockSpec((block_rows, hidden), lambda step, base_ref: (part * blocks + step, 0)),
    ] + [anywhere] * len(pieces)

    def part_block(copy):
        return pl.BlockSpec(
            (block_rows, width + 128),
            lambda step, base_ref: (jnp.clip(step - copy * per_copy, 0, per_copy - 1), 0),
        )

    out_specs = [part_block(copy) for copy in range(copy_count)] + [
        pl.BlockSpec((block_rows, width), here),
        pl.BlockSpec((block_rows, hidden), here),
        pl.BlockSpec((block_rows, hidden), here),
        pl.BlockSpec((block_rows, hidden), here),
    ]
    hidden_shape = jax.ShapeDtypeStruct((total_rows, hidden), bf16)
    out_shape = [
        jax.ShapeDtypeStruct((per_copy * block_rows, width + 128), bf16)
    ] * copy_count + [
        jax.ShapeDtypeStruct((total_rows, width), bf16),
        hidden_shape,
        hidden_shape,
        hidden_shape,
    ]
    aliases = {}
    if kept:
        aliases = {
            1 + len(in_specs) + number: copy_count + number for number in range(len(kept))
        }
    in_specs += [anywhere] * len(kept)
    most_pieces = max(len(block) for block in plan)
    count = blocks * block_rows
    outs = pl.pallas_call(
        functools.partial(expert_kernel, plan, copy_count, width),
        out_shape=out_shape,
        grid_spec=pltpu.PrefetchScalarGridSpec(
            num_scalar_prefetch=1,
            grid=(blocks,),
            in_specs=in_specs,
            out_specs=out_specs,
            scratch_shapes=[
                pltpu.VMEM((2, block_rows, width), bf16),
                pltpu.VMEM((width, hidden), bf16),
                pltpu.VMEM((width, hidden), bf16),
                pltpu.VMEM((block_rows, experts), f32),
                pltpu.SemaphoreType.DMA((2, most_pieces)),
                pltpu.SemaphoreType.DMA((owned,)),
                pltpu.SemaphoreType.DMA((owned,)),
            ],
        ),
        input_output_aliases=aliases,
        compiler_params=pltpu.CompilerParams(vmem_limit_bytes=vmem_limit),
        cost_estimate=pl.CostEstimate(
            flops=8 * count * width * hidden,
            bytes_accessed=4 * width * hidden + 8 * count * width,
            transcendentals=count * hidden,
        ),
    )(base, mask, router, w_gate, w_up, back, *pieces, *kept)
    return list(outs[:copy_count]), list(outs[copy_count:])


def down_kernel(copy_count, gated_ref, down_ref, *refs):
    total = None
    for number in range(down_ref.shape[0]):
        hidden_width = down_ref.shape[1]
        here = slice(number * hidden_width, (number + 1) * hidden_width)
        part = mm(gated_ref[:, here], down_ref[number])
        total = part if total is None else total + part
    for copy, out_ref in enumerate(refs[-copy_count:]):

        @pl.when(pl.program_id(0) == copy)
        def _(out_ref=out_ref):
            out_ref[...] = total.astype(bf16)


def down_products(place, calls, copy_count, gated, w_down, tokens):
    owned, hidden_width, width = w_down.shape
    block = gated.shape[0] // (calls * copy_count)
    return pl.pallas_call(
        functools.partial(down_kernel, copy_count),
        out_shape=[jax.ShapeDtypeStruct((block, width), bf16)] * copy_count,
        grid=(copy_count,),
        in_specs=[
            pl.BlockSpec(
                (block, owned * hidden_width), lambda step: (place * copy_count + step, 0)
            ),
            pl.BlockSpec((owned, hidden_width, width), lambda step: (0, 0, 0)),
        ]
        + [pl.BlockSpec(memory_space=pl.ANY)] * len(tokens),
        out_specs=[pl.BlockSpec((block, width), lambda step: (0, 0))] * copy_count,
        compiler_params=pltpu.CompilerParams(vmem_limit_bytes=vmem_limit),
        cost_estimate=pl.CostEstimate(
            flops=2 * block * copy_count * width * owned * hidden_width,
            bytes_accessed=4 * block * copy_count * width,
            transcendentals=0,
        ),
    )(gated, w_down, *tokens)


def product_kernel(left_ref, right_ref, *refs):
    refs[-1][0] = t_mm(left_ref[...], right_ref[...])


def expert_grads(left, right, owned, tokens):
    total_rows = left.shape[0]
    whole = lambda count: pl.BlockSpec(
        (total_rows, count), lambda step: (0, 0), pipeline_mode=pl.Buffered(1)
    )
    cut = lambda count: pl.BlockSpec((total_rows, count), lambda step: (0, step))
    if left.shape[1] > right.shape[1]:
        out = (left.shape[1], right.shape[1] // owned)
        specs = [whole(out[0]), cut(out[1])]
    else:
        out = (left.shape[1] // owned, right.shape[1])
        specs = [cut(out[0]), whole(out[1])]
    return pl.pallas_call(
        product_kernel,
        grid=(owned,),
        out_shape=jax.ShapeDtypeStruct((owned,) + out, f32),
        in_specs=specs + [pl.BlockSpec(memory_space=pl.ANY)] * len(tokens),
        out_specs=pl.BlockSpec((1,) + out, lambda step: (step, 0, 0)),
        compiler_params=pltpu.CompilerParams(vmem_limit_bytes=vmem_limit),
        cost_estimate=pl.CostEstimate(
            flops=2 * total_rows * owned * out[0] * out[1],
            bytes_accessed=4 * owned * out[0] * out[1] + 4 * total_rows * max(out),
            transcendentals=0,
        ),
    )(left, right, *tokens)


def kernel_params():
    return pltpu.CompilerParams(vmem_limit_bytes=vmem_limit)


def in_vmem(count):
    return [pl.BlockSpec(memory_space=pltpu.VMEM)] * count


def as_row(columns):
    return columns.T[:8]


def as_columns(rows):
    count = rows.shape[1]
    return jnp.concatenate([rows, jnp.zeros((120, count), rows.dtype)], axis=0).T


def in_lanes(*columns):
    lane = lax.broadcasted_iota(jnp.int32, (columns[0].shape[0], 128), 1)
    total = jnp.zeros(lane.shape, f32)
    for number, column in enumerate(columns):
        total = jnp.where(lane == number, column, total)
    return total


def summed_rows(own_ref, arrived_refs, own_rows):
    total = as_columns(own_ref[...])
    count = total.shape[0] // own_rows
    places = len(arrived_refs) + 1
    for place, arrived_ref in enumerate(arrived_refs, 1):
        arrived = as_columns(arrived_ref[...])
        blocks = [
            arrived[other * own_rows : (other + 1) * own_rows]
            for other in ((block // places) * places + ((block % places) ^ place) for block in range(count))
        ]
        total = total + jnp.concatenate(blocks, axis=0)
    return total


def project_kernel(
    rows_ref, gain_ref, query_ref, key_ref, value_ref, normed_ref, q_ref, k_ref, v_ref, squares_ref, sums
):
    step = pl.program_id(0)

    @pl.when(step == 0)
    def _():
        rows = rows_ref[...].astype(f32)
        normed_ref[...] = (rows * rms_scale(rows) * gain_ref[...]).astype(bf16)

    normed = normed_ref[...]
    query, key = mm(normed, query_ref[...]), mm(normed, key_ref[...])
    q_ref[...] = query
    k_ref[...] = key
    v_ref[...] = mm(normed, value_ref[...]).astype(bf16)
    here = in_lanes(
        jnp.sum(query * query, axis=1, keepdims=True), jnp.sum(key * key, axis=1, keepdims=True)
    )
    sums[...] = jnp.where(step == 0, 0.0, sums[...]) + here
    squares_ref[...] = as_row(sums[...])


def project(rows, gain, w_query, w_key, w_value):
    count, width = rows.shape
    local_width = w_query.shape[1]
    block = min(256, local_width)
    weight = pl.BlockSpec((width, block), lambda step: (0, step))
    whole = lambda *shape: pl.BlockSpec(shape, lambda step: (0, 0))
    out = pl.BlockSpec((count, block), lambda step: (0, step))
    raw = jax.ShapeDtypeStruct((count, local_width), f32)
    return pl.pallas_call(
        project_kernel,
        grid=(local_width // block,),
        out_shape=[
            jax.ShapeDtypeStruct((count, width), bf16),
            raw,
            raw,
            jax.ShapeDtypeStruct((count, local_width), bf16),
            jax.ShapeDtypeStruct((8, count), f32),
        ],
        in_specs=[whole(count, width), whole(1, width), weight, weight, weight],
        out_specs=[whole(count, width), out, out, out, whole(8, count)],
        scratch_shapes=[pltpu.VMEM((count, 128), f32)],
        compiler_params=kernel_params(),
    )(rows, gain[None], w_query, w_key, w_value)


def turn_kernel(
    own_rows, width, partners, q_ref, k_ref, v_ref, q_gain_ref, k_gain_ref, cos_ref, sin_ref, own_ref, *refs
):
    packed_ref, scales_ref = refs[partners:]
    squares = summed_rows(own_ref, refs[:partners], own_rows)
    scales = lax.rsqrt(squares / width + eps)
    scales_ref[...] = scales
    pairs, rows, wide = packed_ref.shape
    size = wide // 3
    heads = q_ref.shape[1] // size
    for pair in range(pairs):
        micro, head = pair // heads, pair % heads
        here = slice(micro * rows, (micro + 1) * rows)
        lanes = slice(head * size, (head + 1) * size)
        for part, (raw_ref, gain_ref) in enumerate(((q_ref, q_gain_ref), (k_ref, k_gain_ref))):
            normed = raw_ref[here, lanes] * scales[here, part : part + 1] * gain_ref[:, lanes]
            turned = normed * cos_ref[...] + turn_half(normed) * sin_ref[...]
            packed_ref[pair, :, part * size : (part + 1) * size] = turned.astype(bf16)
        packed_ref[pair, :, 2 * size :] = v_ref[here, lanes]


def turn_and_pack(query, key, value, gains, cosine, sine, squares, arrived, own_rows, width, pairs):
    rows, size = cosine.shape
    count = query.shape[0]
    return pl.pallas_call(
        functools.partial(turn_kernel, own_rows, width, len(arrived)),
        out_shape=[
            jax.ShapeDtypeStruct((pairs, rows, 3 * size), bf16),
            jax.ShapeDtypeStruct((count, 128), f32),
        ],
        in_specs=in_vmem(8 + len(arrived)),
        out_specs=in_vmem(2),
        compiler_params=kernel_params(),
    )(query, key, value, *gains, cosine, sine, squares, *arrived)


def unturn_kernel(
    packed_ref, q_ref, k_ref, q_gain_ref, k_gain_ref, cos_ref, sin_ref, scales_ref,
    q_grad_ref, k_grad_ref, v_grad_ref, dots_ref, gains_ref,
):
    pairs, rows, wide = packed_ref.shape
    size = wide // 3
    heads = q_ref.shape[1] // size
    gains_ref[...] = jnp.zeros_like(gains_ref)
    dots = []
    for micro in range(pairs // heads):
        here = slice(micro * rows, (micro + 1) * rows)
        sums = [jnp.zeros((rows, 1), f32)] * 2
        for head in range(heads):
            lanes = slice(head * size, (head + 1) * size)
            refs = ((q_ref, q_gain_ref, q_grad_ref), (k_ref, k_gain_ref, k_grad_ref))
            for part, (raw_ref, gain_ref, out_ref) in enumerate(refs):
                grad = packed_ref[micro * heads + head, :, part * size : (part + 1) * size]
                grad = grad.astype(f32)
                grad = grad * cos_ref[...] + turn_back(grad * sin_ref[...])
                out_ref[here, lanes] = grad
                product = grad * raw_ref[here, lanes]
                sums[part] = sums[part] + jnp.sum(
                    product * gain_ref[:, lanes], axis=1, keepdims=True
                )
                gains_ref[part : part + 1, lanes] += jnp.sum(
                    product * scales_ref[here, part : part + 1], axis=0, keepdims=True
                )
            v_grad_ref[here, lanes] = packed_ref[micro * heads + head, :, 2 * size :]
        dots.append(in_lanes(*sums))
    dots_ref[...] = as_row(jnp.concatenate(dots, axis=0))


def unturn(packed, query, key, gains, cosine, sine, scales):
    count, local_width = query.shape
    raw = jax.ShapeDtypeStruct((count, local_width), f32)
    return pl.pallas_call(
        unturn_kernel,
        out_shape=[
            raw,
            raw,
            jax.ShapeDtypeStruct((count, local_width), bf16),
            jax.ShapeDtypeStruct((8, count), f32),
            jax.ShapeDtypeStruct((8, local_width), f32),
        ],
        in_specs=in_vmem(8),
        out_specs=in_vmem(5),
        compiler_params=kernel_params(),
    )(packed, query, key, *gains, cosine, sine, scales)


def norm_back_kernel(
    own_rows, width, partners, q_grad_ref, k_grad_ref, q_ref, k_ref, q_gain_ref, k_gain_ref, scales_ref, own_ref, *refs
):
    outs = refs[partners:]
    dots = summed_rows(own_ref, refs[:partners], own_rows)
    refs = ((q_grad_ref, q_ref, q_gain_ref), (k_grad_ref, k_ref, k_gain_ref))
    for part, (grad_ref, raw_ref, gain_ref) in enumerate(refs):
        scale = scales_ref[:, part : part + 1]
        dot = dots[:, part : part + 1]
        grad = scale * gain_ref[...] * grad_ref[...] - raw_ref[...] * (scale**3 * dot / width)
        outs[part][...] = grad.astype(bf16)


def norm_back(q_grad, k_grad, query, key, gains, scales, dots, arrived, own_rows, width):
    count, local_width = query.shape
    return pl.pallas_call(
        functools.partial(norm_back_kernel, own_rows, width, len(arrived)),
        out_shape=[jax.ShapeDtypeStruct((count, local_width), bf16)] * 2,
        in_specs=in_vmem(8 + len(arrived)),
        out_specs=in_vmem(2),
        compiler_params=kernel_params(),
    )(q_grad, k_grad, query, key, *gains, scales, dots, *arrived)


def project_back_kernel(
    q_ref, k_ref, v_ref, rows_ref, scale_ref, query_ref, key_ref, value_ref, out_ref, gain_ref
):
    part = (
        mm_t(q_ref[...], query_ref[...])
        + mm_t(k_ref[...], key_ref[...])
        + mm_t(v_ref[...], value_ref[...])
    )
    out_ref[...] = part.astype(bf16)
    rows = rows_ref[...].astype(f32) * scale_ref[...]
    gain_ref[...] = jnp.sum(part * rows, axis=0, keepdims=True)


def project_back(query_grad, key_grad, value_grad, rows, scale, w_query, w_key, w_value):
    count, width = rows.shape
    local_width = w_query.shape[1]
    block = min(512, width)
    whole = lambda *shape: pl.BlockSpec(shape, lambda step: (0, 0))
    weight = pl.BlockSpec((block, local_width), lambda step: (step, 0))
    cut = pl.BlockSpec((count, block), lambda step: (0, step))
    return pl.pallas_call(
        project_back_kernel,
        grid=(width // block,),
        out_shape=[
            jax.ShapeDtypeStruct((count, width), bf16),
            jax.ShapeDtypeStruct((1, width), f32),
        ],
        in_specs=[
            whole(count, local_width),
            whole(count, local_width),
            whole(count, local_width),
            cut,
            whole(count, 1),
            weight,
            weight,
            weight,
        ],
        out_specs=[cut, pl.BlockSpec((1, block), lambda step: (0, step))],
        compiler_params=kernel_params(),
    )(query_grad, key_grad, value_grad, rows, scale, w_query, w_key, w_value)


def rows_back_kernel(
    parts_ref, residual_ref, normed_ref, mask_ref, router_ref, gain_ref, upstream_ref,
    grad_ref, low_ref, router_grad_ref, gain_grad_ref,
):
    width = residual_ref.shape[1]
    experts = router_ref.shape[1]
    total = parts_ref[0].astype(f32)
    for number in range(1, parts_ref.shape[0]):
        total = total + parts_ref[number].astype(f32)
    normed = normed_ref[...]
    logits = mm(normed, router_ref[...])
    probs = jnp.exp(logits - jnp.max(logits, axis=1, keepdims=True))
    probs = probs / jnp.sum(probs, axis=1, keepdims=True)
    prob_grad = total[:, width : width + experts] * mask_ref[:, :experts].astype(f32)
    logit_grad = probs * (prob_grad - jnp.sum(prob_grad * probs, axis=1, keepdims=True))
    logit_grad = logit_grad.astype(bf16)
    grad = total[:, :width] + mm_t(logit_grad, router_ref[...])
    router_grad_ref[...] = t_mm(logit_grad, normed)
    residual = residual_ref[...]
    scale = rms_scale(residual)
    scaled = residual * scale
    gain_grad_ref[...] = jnp.sum(grad * scaled, axis=0, keepdims=True)
    weighted = grad * gain_ref[...]
    back = (
        upstream_ref[...].astype(f32)
        + scale * weighted
        - scaled * (scale**2 * jnp.mean(weighted * residual, axis=1, keepdims=True))
    )
    grad_ref[...] = back
    low_ref[...] = back.astype(bf16)


def rows_back(parts, residual, normed, mask, router, gain, upstream):
    rows, width = residual.shape
    return pl.pallas_call(
        rows_back_kernel,
        out_shape=[
            jax.ShapeDtypeStruct((rows, width), f32),
            jax.ShapeDtypeStruct((rows, width), bf16),
            jax.ShapeDtypeStruct((router.shape[1], width), f32),
            jax.ShapeDtypeStruct((1, width), f32),
        ],
        in_specs=in_vmem(7),
        out_specs=in_vmem(4),
        compiler_params=kernel_params(),
    )(parts, residual, normed, mask, router, gain[None], upstream)


def attention_forward(query, key, value, causal, scale):
    scores = mm_t(query, key) * scale
    scores = jnp.where(causal, scores, masked_score)
    highest = jnp.max(scores, axis=1, keepdims=True)
    log_total = highest + jnp.log(jnp.sum(jnp.exp(scores - highest), axis=1, keepdims=True))
    probs_low = jnp.exp(scores - log_total).astype(bf16)
    return mm(probs_low, value).astype(bf16), log_total


def attention_backward(query, key, value, log_total, grad, causal, scale):
    scores = mm_t(query, key) * scale
    scores = jnp.where(causal, scores, masked_score)
    probs = jnp.exp(scores - log_total)
    probs_low = probs.astype(bf16)
    dprob = mm_t(grad, value)
    score_grad = (probs * (dprob - jnp.sum(dprob * probs, axis=1, keepdims=True))).astype(bf16)
    return (
        (mm(score_grad, key) * scale).astype(bf16),
        (t_mm(score_grad, query) * scale).astype(bf16),
        t_mm(probs_low, grad).astype(bf16),
    )


def shards(
    tokens,
    out_grad,
    routes,
    norm1_gain,
    w_query,
    w_key,
    w_value,
    query_gain,
    key_gain,
    w_output,
    norm2_gain,
    w_router,
    w_gate,
    w_up,
    w_down,
):
    micro_count, rows_here, width = tokens.shape
    local_width = w_query.shape[1]
    heads_here, head_size = query_gain.shape
    experts = w_router.shape[1]
    groups = lax.axis_size("expert")
    tensor_count = lax.axis_size("tensor")
    owned, _, hidden_width = w_gate.shape
    own_rows = rows_here // tensor_count
    flat_rows = micro_count * rows_here
    score_scale = head_size ** (-0.5)
    expert_at = lax.axis_index("expert")
    tensor_at = lax.axis_index("tensor")

    expert_bits = bits_of(groups)
    tensor_bits = bits_of(tensor_count)
    tensor_steps = [("tensor", bit) for bit in tensor_bits]
    tensor_order = partner_order(tensor_bits)

    def by_partner(operand):
        return jnp.concatenate(
            [
                lax.dynamic_slice_in_dim(operand, (tensor_at ^ place) * own_rows, own_rows, axis=1)
                for place in tensor_order
            ],
            axis=1,
        )

    def in_sequence(operand):
        place_of = jnp.asarray(
            [tensor_order.index(place) for place in range(tensor_count)], jnp.int32
        )
        return jnp.concatenate(
            [
                lax.dynamic_slice_in_dim(
                    operand, place_of[tensor_at ^ place] * own_rows, own_rows, axis=1
                )
                for place in range(tensor_count)
            ],
            axis=1,
        )

    pairs = micro_count * heads_here
    per_device = max(1, pairs // groups)
    copies = max(1, groups // pairs)

    def to_heads(operand, work=None):
        wide = operand.shape[3]
        return pairs_to_heads(
            operand.transpose(0, 2, 1, 3).reshape(pairs, rows_here, wide), work
        )

    def pairs_to_heads(blocks, work=None):
        wide = blocks.shape[2]
        if copies > 1:
            blocks = jnp.repeat(blocks, copies, axis=0)
        arrived = lax.all_to_all(blocks, "expert", split_axis=0, concat_axis=0, tiled=True)
        if work is not None:
            arrived = after(arrived, *work(blocks))
        blocks = arrived.reshape(groups, per_device, rows_here, wide)
        return blocks.transpose(1, 0, 2, 3).reshape(per_device, groups * rows_here, wide)

    def pairs_from_heads(operand, others=()):
        wide = operand.shape[2]
        blocks = operand.reshape(per_device, groups, rows_here, wide).transpose(1, 0, 2, 3)
        blocks = blocks.reshape(groups * per_device, rows_here, wide)
        blocks = lax.all_to_all(blocks, "expert", split_axis=0, concat_axis=0, tiled=True)
        if others:
            blocks = after(blocks, *others)
        if copies > 1:
            blocks = blocks[::copies]
        return blocks

    def from_heads(operand, others=()):
        blocks = pairs_from_heads(operand, others)
        wide = blocks.shape[2]
        return blocks.reshape(micro_count, heads_here, rows_here, wide).transpose(0, 2, 1, 3)

    row_number = jnp.arange(own_rows, dtype=jnp.int32)
    row_in_block = jnp.concatenate(
        [(tensor_at ^ place) * own_rows + row_number for place in tensor_order]
    )
    row_pos = expert_at * rows_here + row_in_block
    frequency = theta_base ** (-(jnp.arange(head_size // 2, dtype=f32) * 2.0 / head_size))
    angles = row_pos.astype(f32)[:, None] * frequency[None, :]
    angles = jnp.concatenate([angles, angles], axis=1)
    cosine = jnp.cos(angles)
    sine = jnp.sin(angles)
    sequence_pos = (
        jnp.arange(groups, dtype=jnp.int32)[:, None] * rows_here + row_in_block[None, :]
    ).reshape(-1)
    causal = sequence_pos[None, :] <= sequence_pos[:, None]

    near, side = 1, tensor_bits[0]
    far = groups // 2
    far_groups = [[2 * place + last for place in range(far)] for last in range(2)]
    copy_count = tensor_count // 2

    def far_exchange(blocks):
        return lax.all_to_all(
            blocks, "expert", split_axis=0, concat_axis=0, axis_index_groups=far_groups, tiled=True
        )

    def gather_far(rows, work=None):
        block = far_exchange(jnp.broadcast_to(rows[None], (far,) + rows.shape))
        if work is not None:
            block = after(block, *work())
        return block.reshape((far * rows.shape[0],) + rows.shape[1:])

    def gather_sides(block, work=None):
        arrived = [swap(block, "expert", near), swap(block, "tensor", side)]
        return after_all(arrived, *work()) if work is not None else arrived

    def gather_diagonal(by_near, by_side):
        half = by_near.shape[0] // 2
        low, high = swap(by_side[:half], "expert", near), swap(by_near[half:], "tensor", side)
        return jnp.concatenate([low, high], axis=0)

    def gather_rest(block, by_near, by_side):
        half = block.shape[0] // 2
        by_both_low = swap(by_side[:half], "expert", near)
        by_both_high = swap(by_near[half:], "tensor", side)
        copies = [[[block, by_near], [by_side, by_both_low, by_both_high]]]
        for bit in tensor_bits[1:]:
            copies = copies + [
                [[swap(piece, "tensor", bit) for piece in call] for call in copy]
                for copy in copies
            ]
        return [[copy[call] for copy in copies] for call in range(2)]

    def add(*terms):
        total = terms[0].astype(f32)
        for term in terms[1:]:
            total = total + term.astype(f32)
        return total

    def reduce_copies(parts, work=None):
        for bit in tensor_bits[1:][::-1]:
            half = len(parts) // 2
            arrived = [swap(part, "tensor", bit) for part in parts[half:]]
            if work is not None and half == 1:
                arrived = after_all(arrived, *work(parts[1]))
            parts = [add(part, other).astype(bf16) for part, other in zip(parts[:half], arrived)]
        return parts[0]

    def reduce_diagonal(second, work=None):
        half, quarter = second.shape[0] // 2, second.shape[0] // 4
        low, high = second[half : half + quarter], second[half + quarter :]
        arrived = [swap(low, "expert", near), swap(high, "tensor", side)]
        return after_all(arrived, *work(low)) if work is not None else arrived

    def side_parts(first, second, from_near, from_side):
        half, quarter = second.shape[0] // 2, second.shape[0] // 4
        near_part = [first[half : half + quarter], add(first[half + quarter :], from_side)]
        side_part = [add(second[:quarter], from_near), second[quarter:half]]
        return [
            jnp.concatenate([part.astype(bf16) for part in parts], axis=0)
            for parts in (near_part, side_part)
        ]

    def reduce_sides(near_part, side_part, work=None):
        arrived = [swap(near_part, "expert", near), swap(side_part, "tensor", side)]
        return after_all(arrived, *work(near_part)) if work is not None else arrived

    def far_block(first, by_near, by_side):
        return add(first[: first.shape[0] // 2], by_near, by_side).astype(bf16)

    def reduce_far(block, work=None):
        parts = far_exchange(block.reshape((far, block.shape[0] // far) + block.shape[1:]))
        if work is not None:
            parts = after(parts, *work(block))
        return parts

    def far_sum(parts):
        return jnp.sum(parts.astype(f32), axis=0)

    high_bits = [bit for bit in expert_bits if bit >= 4]
    low_places = [place for place in range(1, min(4, groups))]

    def columns_of(operand, low_place):
        block = operand.shape[1] // groups
        return jnp.concatenate(
            [
                lax.dynamic_slice_in_dim(
                    operand, (expert_at ^ low_place ^ place) * block, block, axis=1
                )
                for place in partner_order(high_bits)
            ],
            axis=1,
        )

    near_count = min(4, groups)
    near_groups = [
        [first + place for place in range(near_count)] for first in range(0, groups, near_count)
    ]

    def near_exchange(operand):
        block = operand.shape[1] // groups
        high = expert_at - expert_at % near_count
        parts = [
            jnp.concatenate(
                [
                    lax.dynamic_slice_in_dim(
                        operand, ((high ^ above) + place) * block, block, axis=1
                    )
                    for above in partner_order(high_bits)
                ],
                axis=1,
            )
            for place in range(near_count)
        ]
        arrived = lax.all_to_all(
            jnp.stack(parts),
            "expert",
            split_axis=0,
            concat_axis=0,
            axis_index_groups=near_groups,
            tiled=True,
        )
        return arrived.reshape(near_count * flat_rows, -1)

    def near_gather(operand):
        return lax.all_gather(
            operand, "expert", axis_index_groups=near_groups, axis=0, tiled=True
        )

    def near_rows(gathered, place):
        return lax.dynamic_slice_in_dim(
            gathered, ((expert_at % 4) ^ place) * flat_rows, flat_rows, axis=0
        )

    def near_swaps(operand):
        return [swap(operand, "expert", place) for place in low_places]

    def halve_product(product):
        return halve_rows(product, [("expert", bit) for bit in high_bits[::-1]], 0, f32)

    grad_rows = lax.dynamic_slice_in_dim(out_grad, tensor_at * own_rows, own_rows, axis=1)
    route_rows = lax.dynamic_slice_in_dim(routes, tensor_at * own_rows, own_rows, axis=1)
    mask_rows = jnp.sum(
        (route_rows[..., None] == jnp.arange(experts, dtype=jnp.int32)).astype(f32), axis=2
    )
    upstream = jnp.concatenate(
        [grad_rows, jnp.pad(mask_rows, ((0, 0), (0, 0), (0, 128 - experts))).astype(bf16)], axis=2
    )
    upstream = upstream.reshape(micro_count * own_rows, width + 128)
    upstream_gathered = lax.all_gather(upstream, ("expert", "tensor"), axis=0, tiled=True)

    tokens_here = by_partner(tokens)
    flat_tokens = tokens_here.reshape(flat_rows, width)
    norm_in, query_raw, key_raw, value_low, squares = project(
        flat_tokens, norm1_gain, w_query, w_key, w_value
    )
    gains = [query_gain.reshape(1, local_width), key_gain.reshape(1, local_width)]
    head_shape = (micro_count, rows_here, heads_here, head_size)

    def from_partners(operand):
        return [swap(operand, "tensor", place) for place in tensor_order[1:]]

    packed, scales = turn_and_pack(
        query_raw,
        key_raw,
        value_low,
        gains,
        cosine,
        sine,
        squares,
        from_partners(squares),
        own_rows,
        width,
        pairs,
    )
    packed = pairs_to_heads(packed)
    head_parts = []
    for number in range(per_device):
        parts = [
            packed[number, :, part * head_size : (part + 1) * head_size] for part in range(3)
        ]
        head_parts.append((parts, attention_forward(*parts, causal, score_scale)))
    attended = from_heads(jnp.stack([out for _, (out, _) in head_parts]))
    attended = attended.reshape(flat_rows, local_width)

    attn_part = mm(attended, w_output).astype(bf16).reshape(micro_count, rows_here, width)
    halves = jnp.split(attn_part, 2, axis=1)
    attn_half = add(halves[0], swap(halves[1], *tensor_steps[-1]))
    attn_rows = halve_rows(attn_half.astype(bf16), tensor_steps[:-1][::-1], 1, f32)
    own_source = tokens_here[:, :own_rows].astype(f32)
    residual = (own_source + attn_rows).reshape(micro_count * own_rows, width)
    norm_out = (residual * rms_scale(residual) * norm2_gain).astype(bf16)

    expert_base = jnp.reshape(expert_at * owned, (1,)).astype(jnp.int32)
    table = []
    for call in range(2):
        for copy_place in partner_order(tensor_bits[1:]):
            for last in range(2):
                for place in range(far):
                    owner = 2 * place + (expert_at % 2 ^ last)
                    table.append(
                        owner * tensor_count + (tensor_at ^ (copy_place ^ (call * side)))
                    )
    table = jnp.stack(table).astype(jnp.int32)
    upstream_made = []

    def upstream_work(call, token):
        def work():
            upstream_made.append(
                upstream_products(
                    call,
                    2,
                    table,
                    upstream_gathered,
                    w_down,
                    [upstream_made[-1][2]] if upstream_made else [],
                    [token],
                )
            )
            return upstream_made[-1][:1]

        return work

    block = gather_far(norm_out, upstream_work(0, norm_out))
    by_near, by_side = gather_sides(block, upstream_work(1, block))
    gathered = gather_rest(block, by_near, by_side)
    upstream_all = upstream_made[-1][2]
    total_rows = micro_count * groups * rows_here
    kept = []

    def expert_rows(call):
        nonlocal kept
        copies = gathered[call]
        rows = sum(piece.shape[0] for piece in copies[0])
        count = min(copy_count, max(1, expert_rows_most // rows))
        all_parts = []
        for part in range(copy_count // count):
            parts, kept = expert_call(
                call * (copy_count // count) + part,
                total_rows,
                part,
                expert_base,
                copies[part * count : (part + 1) * count],
                rows // 2,
                upstream_made[call][1],
                w_router,
                w_gate,
                w_up,
                upstream_made[call][0],
                kept,
            )
            all_parts += parts
        return all_parts

    made = {}

    def down_work(call):
        def work(token):
            tokens = token if isinstance(token, list) else [token]
            made[call] = down_products(call, 2, copy_count, kept[1], w_down, tokens)
            return list(made[call][:1])

        return work

    def grad_work(name, left, right, *others):
        def work(token):
            tokens = token if isinstance(token, list) else [token]
            made[name] = expert_grads(left, right, owned, tokens)
            return [made[name], *others]

        return work

    attended_gathered = near_gather(attended)
    first = expert_rows(0)
    norm_in_gathered = near_exchange(after(norm_in, first[0]))
    first = reduce_copies(first)
    second = expert_rows(1)
    second = reduce_copies(after_all(second, norm_in_gathered))
    near_part, side_part = side_parts(first, second, *reduce_diagonal(second, lambda token: down_work(0)([token, first])))
    arrived = reduce_sides(
        near_part,
        side_part,
        lambda token: down_work(1)(token) + grad_work("down", kept[1], upstream_all)(token),
    )
    out_first, out_second = (reduce_copies(made[call]) for call in range(2))
    out_diagonal = reduce_diagonal(out_second)
    row_parts = reduce_far(
        far_block(first, *arrived),
        lambda token: [out_first, out_second],
    )
    residual_grad, residual_low, router_part, second_gain_part = rows_back(
        after(row_parts, attended_gathered),
        residual,
        norm_out,
        upstream[:, width:],
        w_router,
        norm2_gain,
        grad_rows.reshape(micro_count * own_rows, width),
    )
    out_sides = reduce_sides(
        *side_parts(out_first, out_second, *after_all(out_diagonal, residual_low))
    )
    residual_grad, residual_low = (
        item.reshape(micro_count, own_rows, width) for item in (residual_grad, residual_low)
    )
    residual_low = jnp.concatenate(
        [residual_low, swap(residual_low, *tensor_steps[0])], axis=1
    )
    residual_low = double_rows(residual_low, tensor_steps[1:], 1).reshape(flat_rows, width)

    attended_grad = mm_t(residual_low, w_output).astype(bf16).reshape(head_shape)
    attended_grad = to_heads(attended_grad, grad_work("up", kept[0], kept[3], *out_sides))
    head_grads = []
    for number in range(per_device):
        parts, (_, log_total) = head_parts[number]
        grads = attention_backward(*parts, log_total, attended_grad[number], causal, score_scale)
        head_grads.append(jnp.concatenate(grads, axis=1))
    residual_gathered = near_exchange(after(residual_low, attended_grad))
    head_grads = after(jnp.stack(head_grads), residual_gathered)
    out_block = far_block(out_first, *after_all(out_sides, attended_grad))
    packed_grad = pairs_from_heads(
        head_grads, grad_work("gate", kept[0], kept[2])(head_grads)
    )
    out_parts = reduce_far(after(out_block, packed_grad))
    normed_q_grad, normed_k_grad, value_grad_low, row_dots, gain_parts = unturn(
        packed_grad, query_raw, key_raw, gains, cosine, sine, scales
    )
    value_arrived = near_swaps(value_grad_low)
    query_grad_low, key_grad_low = norm_back(
        normed_q_grad,
        normed_k_grad,
        query_raw,
        key_raw,
        gains,
        scales,
        row_dots,
        [after(dots, out_parts) for dots in from_partners(row_dots)],
        own_rows,
        width,
    )
    query_arrived = near_swaps(query_grad_low)
    norm_in_there = after(norm_in_gathered, query_grad_low)
    norm_in_near = jnp.concatenate(
        [near_rows(norm_in_there, place) for place in range(near_count)], axis=0
    )

    def near_product(own, arrived, *others):
        right = jnp.concatenate([own] + after_all(arrived, *others), axis=0)
        return t_mm(norm_in_near, right).astype(bf16)

    value_product = near_product(value_grad_low, value_arrived, query_grad_low)
    query_arrived = after_all(query_arrived, value_product)
    key_arrived = near_swaps(after(key_grad_low, *query_arrived))
    query_product = near_product(query_grad_low, query_arrived)
    key_arrived = after_all(key_arrived, query_product)
    key_product = near_product(key_grad_low, key_arrived)
    grad_value, grad_query = (halve_product(item) for item in (value_product, query_product))
    grad_key = halve_product(key_product)
    output_product = t_mm(residual_gathered, after(attended_gathered, query_grad_low))
    grad_output = halve_product(output_product.astype(bf16)).T

    scale_in = rms_scale(tokens_here.astype(f32))
    norm_in_part, first_gain_part = project_back(
        after(query_grad_low, value_product),
        key_grad_low,
        value_grad_low,
        flat_tokens,
        scale_in.reshape(flat_rows, 1),
        w_query,
        w_key,
        w_value,
    )
    norm_in_grad = halve_rows(
        norm_in_part.reshape(micro_count, rows_here, width),
        tensor_steps[::-1],
        1,
        f32,
    )
    own_scale = scale_in[:, :own_rows]
    weighted_in = norm_in_grad * norm1_gain
    tokens_grad = (
        residual_grad
        + own_scale * weighted_in
        - own_source * own_scale**3 * jnp.mean(weighted_in * own_source, axis=2, keepdims=True)
    )
    tokens_low = tokens_grad.astype(bf16)
    tokens_grad = in_sequence(double_rows(tokens_low, tensor_steps, 1)).astype(f32)

    out_rows = far_sum(after(out_parts, tokens_low))
    layer_out = (residual + out_rows).astype(bf16)
    layer_out = layer_out.reshape(micro_count, own_rows, tensor_count, -1).transpose(2, 0, 1, 3)
    layer_out = lax.all_to_all(layer_out, "tensor", split_axis=0, concat_axis=0, tiled=True)
    layer_out = layer_out.transpose(1, 0, 2, 3).reshape(micro_count, rows_here, -1)

    column_block = width // groups

    def reduce_small(rows):
        rows = jnp.pad(rows, ((0, -rows.shape[0] % 16), (0, 0))).astype(bf16)
        rows = rows.reshape(-1, groups, column_block).transpose(1, 0, 2)
        rows = lax.all_to_all(rows, "expert", split_axis=0, concat_axis=0, tiled=True)
        rows = jnp.sum(rows.astype(f32), axis=0).astype(bf16)
        return sum_over(rows, tensor_steps).astype(f32)

    head_block = head_size // groups
    head_gains = gain_parts[:2].reshape(2 * heads_here, groups, head_block)
    head_gains = head_gains.transpose(1, 0, 2).reshape(groups, 2 * heads_here * head_block)
    head_gains = jnp.pad(head_gains, ((0, 0), (0, column_block - head_gains.shape[1])))
    head_rows = jnp.where(
        jnp.arange(tensor_count, dtype=jnp.int32)[:, None] == tensor_at,
        head_gains.reshape(1, width),
        0.0,
    )
    small = reduce_small(
        after(
            jnp.concatenate(
                [router_part, second_gain_part, first_gain_part, head_rows], axis=0
            ),
            tokens_low,
        )
    )
    grad_router = small[:experts].T
    own_heads = lax.dynamic_slice_in_dim(small, experts + 2 + tensor_at, 1, axis=0)
    own_heads = own_heads[0, : 2 * heads_here * head_block].reshape(2, heads_here, head_block)


    return (
        layer_out,
        tokens_grad,
        small[experts + 1],
        grad_query,
        grad_key,
        grad_value,
        own_heads[0],
        own_heads[1],
        grad_output,
        small[experts],
        grad_router,
        made["gate"],
        made["up"],
        made["down"],
    )


def solution(mesh):
    placed = (
        P(None, "expert", None),
        P(None, "expert", None),
        P(None, "expert", None),
        P(),
        P(None, "tensor"),
        P(None, "tensor"),
        P(None, "tensor"),
        P("tensor", None),
        P("tensor", None),
        P("tensor", None),
        P(),
        P(),
        P("expert", None, "tensor"),
        P("expert", None, "tensor"),
        P("expert", "tensor", None),
    )
    return jax.shard_map(
        shards,
        mesh=mesh,
        in_specs=placed,
        out_specs=(
            P(None, "expert", "tensor"),
            P(None, "expert", None),
            P("expert"),
            P("expert", "tensor"),
            P("expert", "tensor"),
            P("expert", "tensor"),
            P("tensor", "expert"),
            P("tensor", "expert"),
            P("tensor", "expert"),
            P("expert"),
            P("expert", None),
            P("expert", None, "tensor"),
            P("expert", None, "tensor"),
            P("expert", "tensor", None),
        ),
        check_vma=False,
    )
```

```python
import functools

import jax
import jax.numpy as jnp
from jax import lax
from jax.experimental import pallas as pl
from jax.experimental.pallas import tpu as pltpu
from jax.sharding import PartitionSpec as P

eps = 1e-05
theta_base = 10000.0
masked_score = -1e30
bf16 = jnp.bfloat16
f32 = jnp.float32
vmem_limit = 56 * 1024 * 1024
expert_rows_most = 1024


def rms_scale(operand):
    return lax.rsqrt(jnp.mean(operand * operand, axis=-1, keepdims=True) + eps)


def turn_half(operand):
    middle = operand.shape[-1] // 2
    return jnp.concatenate([-operand[..., middle:], operand[..., :middle]], axis=-1)


def turn_back(operand):
    middle = operand.shape[-1] // 2
    return jnp.concatenate([operand[..., middle:], -operand[..., :middle]], axis=-1)


def bits_of(count):
    bits = []
    bit = count // 2
    while bit:
        bits.append(bit)
        bit //= 2
    return bits


def partner_order(bits):
    order = [0]
    for bit in bits:
        order = order + [place ^ bit for place in order]
    return order


def swap(operand, axis_name, bit):
    count = lax.axis_size(axis_name)
    return lax.ppermute(operand, axis_name, [(i, i ^ bit) for i in range(count)])


def double_rows(operand, steps, axis):
    for axis_name, bit in steps:
        operand = jnp.concatenate([operand, swap(operand, axis_name, bit)], axis=axis)
    return operand


def halve_rows(operand, steps, axis, last=bf16):
    for number, (axis_name, bit) in enumerate(steps):
        half = operand.shape[axis] // 2
        kept = lax.slice_in_dim(operand, 0, half, axis=axis)
        sent = lax.slice_in_dim(operand, half, 2 * half, axis=axis)
        total = kept.astype(f32) + swap(sent, axis_name, bit).astype(f32)
        operand = total if number == len(steps) - 1 and last == f32 else total.astype(bf16)
    return operand


def sum_over(operand, steps):
    for axis_name, bit in steps:
        operand = operand + swap(operand, axis_name, bit)
    return operand


def sum_over_rows(operand, steps, own_rows):
    shape = operand.shape
    blocked = operand.reshape((-1,) + (2,) * len(steps) + (own_rows,))
    for number, (axis_name, bit) in enumerate(steps):
        blocked = blocked + jnp.flip(swap(blocked, axis_name, bit), axis=len(steps) - number)
    return blocked.reshape(shape)


def mm(left, right):
    return jnp.dot(left, right, preferred_element_type=f32)


def mm_t(left, right):
    return lax.dot_general(left, right, (((1,), (1,)), ((), ())), preferred_element_type=f32)


def t_mm(left, right):
    return lax.dot_general(left, right, (((0,), (0,)), ((), ())), preferred_element_type=f32)


def after(operand, *others):
    def nothing(*refs):
        pass

    anywhere = pl.BlockSpec(memory_space=pl.ANY)
    return pl.pallas_call(
        nothing,
        out_shape=jax.ShapeDtypeStruct(operand.shape, operand.dtype),
        in_specs=[anywhere] * (1 + len(others)),
        out_specs=anywhere,
        input_output_aliases={0: 0},
    )(operand, *others)


def after_all(operands, *others):
    return [after(operand, *others) for operand in operands] if others else list(operands)


def upstream_kernel(place, blocks, width, table_ref, down_ref, gathered_ref, *refs):
    back_ref, mask_ref, rows_ref, sems = refs[-4:]
    own_rows = rows_ref.shape[0] // blocks

    @pl.when(pl.program_id(0) == 0)
    def _():
        copies = []
        for number in range(blocks):
            start = pl.multiple_of(table_ref[place * blocks + number] * own_rows, own_rows)
            source = gathered_ref.at[pl.ds(start, own_rows)]
            there = pl.ds(number * own_rows, own_rows)
            copies.append(
                pltpu.make_async_copy(
                    source.at[:, pl.ds(0, width)], rows_ref.at[there], sems.at[0, number]
                )
            )
            copies.append(
                pltpu.make_async_copy(
                    source.at[:, pl.ds(width, 128)], mask_ref.at[there], sems.at[1, number]
                )
            )
        for copy in copies:
            copy.start()
        for copy in copies:
            copy.wait()

    back_ref[...] = mm_t(rows_ref[...], down_ref[0])


def upstream_products(place, calls, table, gathered, w_down, kept, tokens):
    owned, hidden_width, width = w_down.shape
    blocks = table.shape[0] // calls
    rows = gathered.shape[0] // calls
    anywhere = pl.BlockSpec(memory_space=pl.ANY)
    others = [gathered] + kept + tokens
    return pl.pallas_call(
        functools.partial(upstream_kernel, place, blocks, width),
        out_shape=[
            jax.ShapeDtypeStruct((rows, owned * hidden_width), f32),
            jax.ShapeDtypeStruct((rows, 128), bf16),
            jax.ShapeDtypeStruct((calls * rows, width), bf16),
        ],
        grid_spec=pltpu.PrefetchScalarGridSpec(
            num_scalar_prefetch=1,
            grid=(owned,),
            in_specs=[pl.BlockSpec((1, hidden_width, width), lambda step, table: (step, 0, 0))]
            + [anywhere] * len(others),
            out_specs=[
                pl.BlockSpec((rows, hidden_width), lambda step, table: (0, step)),
                pl.BlockSpec((rows, 128), lambda step, table: (0, 0)),
                pl.BlockSpec((rows, width), lambda step, table: (place, 0)),
            ],
            scratch_shapes=[pltpu.SemaphoreType.DMA((2, blocks))],
        ),
        input_output_aliases={3: 2} if kept else {},
        compiler_params=pltpu.CompilerParams(vmem_limit_bytes=vmem_limit),
        cost_estimate=pl.CostEstimate(
            flops=2 * rows * width * owned * hidden_width,
            bytes_accessed=8 * rows * width,
            transcendentals=0,
        ),
    )(table, w_down, *others)


def expert_kernel(
    plan, copy_count, width, base_ref, mask_ref, router_ref, gate_ref, up_ref, back_ref, *refs
):
    piece_count = sum(len(block) for block in plan)
    piece_refs = refs[:piece_count]
    part_refs = refs[-11 - copy_count : -11]
    copy_ref, gated_ref, gate_back_ref, up_back_ref = refs[-11:-7]
    rows, gates, ups, probs, row_sems, gate_sems, up_sems = refs[-7:]
    step = pl.program_id(0)
    experts = router_ref.shape[1]
    owned, _, hidden_width = gate_ref.shape

    def row_copies(block):
        copies, start = [], 0
        first = sum(len(item) for item in plan[:block])
        for number in range(len(plan[block])):
            piece_ref = piece_refs[first + number]
            count = piece_ref.shape[0]
            copies.append(
                pltpu.make_async_copy(
                    piece_ref,
                    rows.at[block % 2, pl.ds(start, count)],
                    row_sems.at[block % 2, number],
                )
            )
            start += count
        return copies

    def weight_copies(number):
        here = pl.ds(number * hidden_width, hidden_width)
        return [
            pltpu.make_async_copy(gate_ref.at[number], gates.at[:, here], gate_sems.at[number]),
            pltpu.make_async_copy(up_ref.at[number], ups.at[:, here], up_sems.at[number]),
        ]

    @pl.when(step == 0)
    def _():
        for copy in row_copies(0):
            copy.start()
        for number in range(owned):
            for copy in weight_copies(number):
                copy.start()

    for block in range(len(plan)):

        @pl.when(step == block)
        def _(block=block):
            for copy in row_copies(block):
                copy.wait()
            if block + 1 < len(plan):
                for copy in row_copies(block + 1):
                    copy.start()

    own_rows = rows[step % 2]
    copy_ref[...] = own_rows
    logits = mm(own_rows, router_ref[...])
    weights = jnp.exp(logits - jnp.max(logits, axis=1, keepdims=True))
    weights = weights / jnp.sum(weights, axis=1, keepdims=True)
    probs[...] = weights * mask_ref[:, :experts].astype(f32)
    lane = lax.broadcasted_iota(jnp.int32, probs.shape, 1)
    slope_lane = lax.broadcasted_iota(jnp.int32, (own_rows.shape[0], 128), 1)

    slopes = jnp.zeros(slope_lane.shape, f32)
    for number in range(owned):
        here = slice(number * hidden_width, (number + 1) * hidden_width)
        owner = base_ref[0] + number

        @pl.when(step == 0)
        def _(number=number):
            for copy in weight_copies(number):
                copy.wait()

        gate = jnp.sum(jnp.where(lane == owner, probs[...], 0.0), axis=1, keepdims=True)
        gate_pre = mm(rows[step % 2], gates[:, here])
        up_pre = mm(rows[step % 2], ups[:, here])
        back = back_ref[:, here]
        sigmoid_gate = 1.0 / (1.0 + jnp.exp(-gate_pre))
        activated = gate_pre * sigmoid_gate
        hidden = activated * up_pre
        gated_ref[:, here] = (gate * hidden).astype(bf16)
        slope = jnp.sum(hidden * back, axis=1, keepdims=True)
        slopes = slopes + jnp.where(slope_lane == owner, slope, 0.0)
        hidden_grad = gate * back
        gate_back_ref[:, here] = (
            hidden_grad * up_pre * (sigmoid_gate * (1.0 + gate_pre * (1.0 - sigmoid_gate)))
        ).astype(bf16)
        up_back_ref[:, here] = (hidden_grad * activated).astype(bf16)
    part = mm_t(gate_back_ref[...], gates[...]) + mm_t(up_back_ref[...], ups[...])
    part = part.astype(bf16)
    per_copy = len(plan) // copy_count
    for copy, part_ref in enumerate(part_refs):

        @pl.when(step // per_copy == copy)
        def _(part_ref=part_ref):
            part_ref[:, :width] = part
            part_ref[:, width:] = slopes.astype(bf16)


def expert_call(
    place, total_rows, part, base, copies, block_rows, mask, router, w_gate, w_up, back, kept
):
    plan, pieces = [], []
    for copy in copies:
        for piece in copy:
            if not plan or sum(item.shape[0] for item in plan[-1]) == block_rows:
                plan.append([])
            plan[-1].append(piece)
            pieces.append(piece)
    copy_count = len(copies)
    per_copy = len(plan) // copy_count
    owned, width, hidden_width = w_gate.shape
    hidden = owned * hidden_width
    experts = router.shape[1]
    blocks = len(plan)
    anywhere = pl.BlockSpec(memory_space=pl.ANY)
    here = lambda step, base_ref: (place * blocks + step, 0)
    in_specs = [
        pl.BlockSpec((block_rows, 128), lambda step, base_ref: (part * blocks + step, 0)),
        pl.BlockSpec((width, experts), lambda step, base_ref: (0, 0)),
        anywhere,
        anywhere,
        pl.BlockSpec((block_rows, hidden), lambda step, base_ref: (part * blocks + step, 0)),
    ] + [anywhere] * len(pieces)

    def part_block(copy):
        return pl.BlockSpec(
            (block_rows, width + 128),
            lambda step, base_ref: (jnp.clip(step - copy * per_copy, 0, per_copy - 1), 0),
        )

    out_specs = [part_block(copy) for copy in range(copy_count)] + [
        pl.BlockSpec((block_rows, width), here),
        pl.BlockSpec((block_rows, hidden), here),
        pl.BlockSpec((block_rows, hidden), here),
        pl.BlockSpec((block_rows, hidden), here),
    ]
    hidden_shape = jax.ShapeDtypeStruct((total_rows, hidden), bf16)
    out_shape = [
        jax.ShapeDtypeStruct((per_copy * block_rows, width + 128), bf16)
    ] * copy_count + [
        jax.ShapeDtypeStruct((total_rows, width), bf16),
        hidden_shape,
        hidden_shape,
        hidden_shape,
    ]
    aliases = {}
    if kept:
        aliases = {
            1 + len(in_specs) + number: copy_count + number for number in range(len(kept))
        }
    in_specs += [anywhere] * len(kept)
    most_pieces = max(len(block) for block in plan)
    count = blocks * block_rows
    outs = pl.pallas_call(
        functools.partial(expert_kernel, plan, copy_count, width),
        out_shape=out_shape,
        grid_spec=pltpu.PrefetchScalarGridSpec(
            num_scalar_prefetch=1,
            grid=(blocks,),
            in_specs=in_specs,
            out_specs=out_specs,
            scratch_shapes=[
                pltpu.VMEM((2, block_rows, width), bf16),
                pltpu.VMEM((width, hidden), bf16),
                pltpu.VMEM((width, hidden), bf16),
                pltpu.VMEM((block_rows, experts), f32),
                pltpu.SemaphoreType.DMA((2, most_pieces)),
                pltpu.SemaphoreType.DMA((owned,)),
                pltpu.SemaphoreType.DMA((owned,)),
            ],
        ),
        input_output_aliases=aliases,
        compiler_params=pltpu.CompilerParams(vmem_limit_bytes=vmem_limit),
        cost_estimate=pl.CostEstimate(
            flops=8 * count * width * hidden,
            bytes_accessed=4 * width * hidden + 8 * count * width,
            transcendentals=count * hidden,
        ),
    )(base, mask, router, w_gate, w_up, back, *pieces, *kept)
    return list(outs[:copy_count]), list(outs[copy_count:])


def down_kernel(copy_count, gated_ref, down_ref, *refs):
    total = None
    for number in range(down_ref.shape[0]):
        hidden_width = down_ref.shape[1]
        here = slice(number * hidden_width, (number + 1) * hidden_width)
        part = mm(gated_ref[:, here], down_ref[number])
        total = part if total is None else total + part
    for copy, out_ref in enumerate(refs[-copy_count:]):

        @pl.when(pl.program_id(0) == copy)
        def _(out_ref=out_ref):
            out_ref[...] = total.astype(bf16)


def down_products(place, calls, copy_count, gated, w_down, tokens):
    owned, hidden_width, width = w_down.shape
    block = gated.shape[0] // (calls * copy_count)
    return pl.pallas_call(
        functools.partial(down_kernel, copy_count),
        out_shape=[jax.ShapeDtypeStruct((block, width), bf16)] * copy_count,
        grid=(copy_count,),
        in_specs=[
            pl.BlockSpec(
                (block, owned * hidden_width), lambda step: (place * copy_count + step, 0)
            ),
            pl.BlockSpec((owned, hidden_width, width), lambda step: (0, 0, 0)),
        ]
        + [pl.BlockSpec(memory_space=pl.ANY)] * len(tokens),
        out_specs=[pl.BlockSpec((block, width), lambda step: (0, 0))] * copy_count,
        compiler_params=pltpu.CompilerParams(vmem_limit_bytes=vmem_limit),
        cost_estimate=pl.CostEstimate(
            flops=2 * block * copy_count * width * owned * hidden_width,
            bytes_accessed=4 * block * copy_count * width,
            transcendentals=0,
        ),
    )(gated, w_down, *tokens)


def product_kernel(left_ref, right_ref, *refs):
    refs[-1][0] = t_mm(left_ref[...], right_ref[...])


def expert_grads(left, right, owned, tokens):
    total_rows = left.shape[0]
    whole = lambda count: pl.BlockSpec(
        (total_rows, count), lambda step: (0, 0), pipeline_mode=pl.Buffered(1)
    )
    cut = lambda count: pl.BlockSpec((total_rows, count), lambda step: (0, step))
    if left.shape[1] > right.shape[1]:
        out = (left.shape[1], right.shape[1] // owned)
        specs = [whole(out[0]), cut(out[1])]
    else:
        out = (left.shape[1] // owned, right.shape[1])
        specs = [cut(out[0]), whole(out[1])]
    return pl.pallas_call(
        product_kernel,
        grid=(owned,),
        out_shape=jax.ShapeDtypeStruct((owned,) + out, f32),
        in_specs=specs + [pl.BlockSpec(memory_space=pl.ANY)] * len(tokens),
        out_specs=pl.BlockSpec((1,) + out, lambda step: (step, 0, 0)),
        compiler_params=pltpu.CompilerParams(vmem_limit_bytes=vmem_limit),
        cost_estimate=pl.CostEstimate(
            flops=2 * total_rows * owned * out[0] * out[1],
            bytes_accessed=4 * owned * out[0] * out[1] + 4 * total_rows * max(out),
            transcendentals=0,
        ),
    )(left, right, *tokens)


def kernel_params():
    return pltpu.CompilerParams(vmem_limit_bytes=vmem_limit)


def in_vmem(count):
    return [pl.BlockSpec(memory_space=pltpu.VMEM)] * count


def as_row(columns):
    return columns.T[:8]


def as_columns(rows):
    count = rows.shape[1]
    return jnp.concatenate([rows, jnp.zeros((120, count), rows.dtype)], axis=0).T


def in_lanes(*columns):
    lane = lax.broadcasted_iota(jnp.int32, (columns[0].shape[0], 128), 1)
    total = jnp.zeros(lane.shape, f32)
    for number, column in enumerate(columns):
        total = jnp.where(lane == number, column, total)
    return total


def summed_rows(own_ref, arrived_refs, own_rows):
    total = as_columns(own_ref[...])
    count = total.shape[0] // own_rows
    places = len(arrived_refs) + 1
    for place, arrived_ref in enumerate(arrived_refs, 1):
        arrived = as_columns(arrived_ref[...])
        blocks = [
            arrived[other * own_rows : (other + 1) * own_rows]
            for other in ((block // places) * places + ((block % places) ^ place) for block in range(count))
        ]
        total = total + jnp.concatenate(blocks, axis=0)
    return total


def project_kernel(
    rows_ref, gain_ref, query_ref, key_ref, value_ref, normed_ref, q_ref, k_ref, v_ref, squares_ref, sums
):
    step = pl.program_id(0)

    @pl.when(step == 0)
    def _():
        rows = rows_ref[...].astype(f32)
        normed_ref[...] = (rows * rms_scale(rows) * gain_ref[...]).astype(bf16)

    normed = normed_ref[...]
    query, key = mm(normed, query_ref[...]), mm(normed, key_ref[...])
    q_ref[...] = query
    k_ref[...] = key
    v_ref[...] = mm(normed, value_ref[...]).astype(bf16)
    here = in_lanes(
        jnp.sum(query * query, axis=1, keepdims=True), jnp.sum(key * key, axis=1, keepdims=True)
    )
    sums[...] = jnp.where(step == 0, 0.0, sums[...]) + here
    squares_ref[...] = as_row(sums[...])


def project(rows, gain, w_query, w_key, w_value):
    count, width = rows.shape
    local_width = w_query.shape[1]
    block = min(256, local_width)
    weight = pl.BlockSpec((width, block), lambda step: (0, step))
    whole = lambda *shape: pl.BlockSpec(shape, lambda step: (0, 0))
    out = pl.BlockSpec((count, block), lambda step: (0, step))
    raw = jax.ShapeDtypeStruct((count, local_width), f32)
    return pl.pallas_call(
        project_kernel,
        grid=(local_width // block,),
        out_shape=[
            jax.ShapeDtypeStruct((count, width), bf16),
            raw,
            raw,
            jax.ShapeDtypeStruct((count, local_width), bf16),
            jax.ShapeDtypeStruct((8, count), f32),
        ],
        in_specs=[whole(count, width), whole(1, width), weight, weight, weight],
        out_specs=[whole(count, width), out, out, out, whole(8, count)],
        scratch_shapes=[pltpu.VMEM((count, 128), f32)],
        compiler_params=kernel_params(),
    )(rows, gain[None], w_query, w_key, w_value)


def turn_kernel(
    own_rows, width, partners, q_ref, k_ref, v_ref, q_gain_ref, k_gain_ref, cos_ref, sin_ref, own_ref, *refs
):
    packed_ref, scales_ref = refs[partners:]
    squares = summed_rows(own_ref, refs[:partners], own_rows)
    scales = lax.rsqrt(squares / width + eps)
    scales_ref[...] = scales
    pairs, rows, wide = packed_ref.shape
    size = wide // 3
    heads = q_ref.shape[1] // size
    for pair in range(pairs):
        micro, head = pair // heads, pair % heads
        here = slice(micro * rows, (micro + 1) * rows)
        lanes = slice(head * size, (head + 1) * size)
        for part, (raw_ref, gain_ref) in enumerate(((q_ref, q_gain_ref), (k_ref, k_gain_ref))):
            normed = raw_ref[here, lanes] * scales[here, part : part + 1] * gain_ref[:, lanes]
            turned = normed * cos_ref[...] + turn_half(normed) * sin_ref[...]
            packed_ref[pair, :, part * size : (part + 1) * size] = turned.astype(bf16)
        packed_ref[pair, :, 2 * size :] = v_ref[here, lanes]


def turn_and_pack(query, key, value, gains, cosine, sine, squares, arrived, own_rows, width, pairs):
    rows, size = cosine.shape
    count = query.shape[0]
    return pl.pallas_call(
        functools.partial(turn_kernel, own_rows, width, len(arrived)),
        out_shape=[
            jax.ShapeDtypeStruct((pairs, rows, 3 * size), bf16),
            jax.ShapeDtypeStruct((count, 128), f32),
        ],
        in_specs=in_vmem(8 + len(arrived)),
        out_specs=in_vmem(2),
        compiler_params=kernel_params(),
    )(query, key, value, *gains, cosine, sine, squares, *arrived)


def unturn_kernel(
    packed_ref, q_ref, k_ref, q_gain_ref, k_gain_ref, cos_ref, sin_ref, scales_ref,
    q_grad_ref, k_grad_ref, v_grad_ref, dots_ref, gains_ref,
):
    pairs, rows, wide = packed_ref.shape
    size = wide // 3
    heads = q_ref.shape[1] // size
    gains_ref[...] = jnp.zeros_like(gains_ref)
    dots = []
    for micro in range(pairs // heads):
        here = slice(micro * rows, (micro + 1) * rows)
        sums = [jnp.zeros((rows, 1), f32)] * 2
        for head in range(heads):
            lanes = slice(head * size, (head + 1) * size)
            refs = ((q_ref, q_gain_ref, q_grad_ref), (k_ref, k_gain_ref, k_grad_ref))
            for part, (raw_ref, gain_ref, out_ref) in enumerate(refs):
                grad = packed_ref[micro * heads + head, :, part * size : (part + 1) * size]
                grad = grad.astype(f32)
                grad = grad * cos_ref[...] + turn_back(grad * sin_ref[...])
                out_ref[here, lanes] = grad
                product = grad * raw_ref[here, lanes]
                sums[part] = sums[part] + jnp.sum(
                    product * gain_ref[:, lanes], axis=1, keepdims=True
                )
                gains_ref[part : part + 1, lanes] += jnp.sum(
                    product * scales_ref[here, part : part + 1], axis=0, keepdims=True
                )
            v_grad_ref[here, lanes] = packed_ref[micro * heads + head, :, 2 * size :]
        dots.append(in_lanes(*sums))
    dots_ref[...] = as_row(jnp.concatenate(dots, axis=0))


def unturn(packed, query, key, gains, cosine, sine, scales):
    count, local_width = query.shape
    raw = jax.ShapeDtypeStruct((count, local_width), f32)
    return pl.pallas_call(
        unturn_kernel,
        out_shape=[
            raw,
            raw,
            jax.ShapeDtypeStruct((count, local_width), bf16),
            jax.ShapeDtypeStruct((8, count), f32),
            jax.ShapeDtypeStruct((8, local_width), f32),
        ],
        in_specs=in_vmem(8),
        out_specs=in_vmem(5),
        compiler_params=kernel_params(),
    )(packed, query, key, *gains, cosine, sine, scales)


def norm_back_kernel(
    own_rows, width, partners, q_grad_ref, k_grad_ref, q_ref, k_ref, q_gain_ref, k_gain_ref, scales_ref, own_ref, *refs
):
    outs = refs[partners:]
    dots = summed_rows(own_ref, refs[:partners], own_rows)
    refs = ((q_grad_ref, q_ref, q_gain_ref), (k_grad_ref, k_ref, k_gain_ref))
    for part, (grad_ref, raw_ref, gain_ref) in enumerate(refs):
        scale = scales_ref[:, part : part + 1]
        dot = dots[:, part : part + 1]
        grad = scale * gain_ref[...] * grad_ref[...] - raw_ref[...] * (scale**3 * dot / width)
        outs[part][...] = grad.astype(bf16)


def norm_back(q_grad, k_grad, query, key, gains, scales, dots, arrived, own_rows, width):
    count, local_width = query.shape
    return pl.pallas_call(
        functools.partial(norm_back_kernel, own_rows, width, len(arrived)),
        out_shape=[jax.ShapeDtypeStruct((count, local_width), bf16)] * 2,
        in_specs=in_vmem(8 + len(arrived)),
        out_specs=in_vmem(2),
        compiler_params=kernel_params(),
    )(q_grad, k_grad, query, key, *gains, scales, dots, *arrived)


def project_back_kernel(
    q_ref, k_ref, v_ref, rows_ref, scale_ref, query_ref, key_ref, value_ref, out_ref, gain_ref
):
    part = (
        mm_t(q_ref[...], query_ref[...])
        + mm_t(k_ref[...], key_ref[...])
        + mm_t(v_ref[...], value_ref[...])
    )
    out_ref[...] = part.astype(bf16)
    rows = rows_ref[...].astype(f32) * scale_ref[...]
    gain_ref[...] = jnp.sum(part * rows, axis=0, keepdims=True)


def project_back(query_grad, key_grad, value_grad, rows, scale, w_query, w_key, w_value):
    count, width = rows.shape
    local_width = w_query.shape[1]
    block = min(512, width)
    whole = lambda *shape: pl.BlockSpec(shape, lambda step: (0, 0))
    weight = pl.BlockSpec((block, local_width), lambda step: (step, 0))
    cut = pl.BlockSpec((count, block), lambda step: (0, step))
    return pl.pallas_call(
        project_back_kernel,
        grid=(width // block,),
        out_shape=[
            jax.ShapeDtypeStruct((count, width), bf16),
            jax.ShapeDtypeStruct((1, width), f32),
        ],
        in_specs=[
            whole(count, local_width),
            whole(count, local_width),
            whole(count, local_width),
            cut,
            whole(count, 1),
            weight,
            weight,
            weight,
        ],
        out_specs=[cut, pl.BlockSpec((1, block), lambda step: (0, step))],
        compiler_params=kernel_params(),
    )(query_grad, key_grad, value_grad, rows, scale, w_query, w_key, w_value)


def rows_back_kernel(
    parts_ref, residual_ref, normed_ref, mask_ref, router_ref, gain_ref, upstream_ref,
    grad_ref, low_ref, router_grad_ref, gain_grad_ref,
):
    width = residual_ref.shape[1]
    experts = router_ref.shape[1]
    total = parts_ref[0].astype(f32)
    for number in range(1, parts_ref.shape[0]):
        total = total + parts_ref[number].astype(f32)
    normed = normed_ref[...]
    logits = mm(normed, router_ref[...])
    probs = jnp.exp(logits - jnp.max(logits, axis=1, keepdims=True))
    probs = probs / jnp.sum(probs, axis=1, keepdims=True)
    prob_grad = total[:, width : width + experts] * mask_ref[:, :experts].astype(f32)
    logit_grad = probs * (prob_grad - jnp.sum(prob_grad * probs, axis=1, keepdims=True))
    logit_grad = logit_grad.astype(bf16)
    grad = total[:, :width] + mm_t(logit_grad, router_ref[...])
    router_grad_ref[...] = t_mm(logit_grad, normed)
    residual = residual_ref[...]
    scale = rms_scale(residual)
    scaled = residual * scale
    gain_grad_ref[...] = jnp.sum(grad * scaled, axis=0, keepdims=True)
    weighted = grad * gain_ref[...]
    back = (
        upstream_ref[...].astype(f32)
        + scale * weighted
        - scaled * (scale**2 * jnp.mean(weighted * residual, axis=1, keepdims=True))
    )
    grad_ref[...] = back
    low_ref[...] = back.astype(bf16)


def rows_back(parts, residual, normed, mask, router, gain, upstream):
    rows, width = residual.shape
    return pl.pallas_call(
        rows_back_kernel,
        out_shape=[
            jax.ShapeDtypeStruct((rows, width), f32),
            jax.ShapeDtypeStruct((rows, width), bf16),
            jax.ShapeDtypeStruct((router.shape[1], width), f32),
            jax.ShapeDtypeStruct((1, width), f32),
        ],
        in_specs=in_vmem(7),
        out_specs=in_vmem(4),
        compiler_params=kernel_params(),
    )(parts, residual, normed, mask, router, gain[None], upstream)


def attention_forward(query, key, value, causal, scale):
    scores = mm_t(query, key) * scale
    scores = jnp.where(causal, scores, masked_score)
    highest = jnp.max(scores, axis=1, keepdims=True)
    log_total = highest + jnp.log(jnp.sum(jnp.exp(scores - highest), axis=1, keepdims=True))
    probs_low = jnp.exp(scores - log_total).astype(bf16)
    return mm(probs_low, value).astype(bf16), log_total


def attention_backward(query, key, value, log_total, grad, causal, scale):
    scores = mm_t(query, key) * scale
    scores = jnp.where(causal, scores, masked_score)
    probs = jnp.exp(scores - log_total)
    probs_low = probs.astype(bf16)
    dprob = mm_t(grad, value)
    score_grad = (probs * (dprob - jnp.sum(dprob * probs, axis=1, keepdims=True))).astype(bf16)
    return (
        (mm(score_grad, key) * scale).astype(bf16),
        (t_mm(score_grad, query) * scale).astype(bf16),
        t_mm(probs_low, grad).astype(bf16),
    )


def shards(
    tokens,
    out_grad,
    routes,
    norm1_gain,
    w_query,
    w_key,
    w_value,
    query_gain,
    key_gain,
    w_output,
    norm2_gain,
    w_router,
    w_gate,
    w_up,
    w_down,
):
    micro_count, rows_here, width = tokens.shape
    local_width = w_query.shape[1]
    heads_here, head_size = query_gain.shape
    experts = w_router.shape[1]
    groups = lax.axis_size("expert")
    tensor_count = lax.axis_size("tensor")
    owned, _, hidden_width = w_gate.shape
    own_rows = rows_here // tensor_count
    flat_rows = micro_count * rows_here
    score_scale = head_size ** (-0.5)
    expert_at = lax.axis_index("expert")
    tensor_at = lax.axis_index("tensor")

    expert_bits = bits_of(groups)
    tensor_bits = bits_of(tensor_count)
    tensor_steps = [("tensor", bit) for bit in tensor_bits]
    tensor_order = partner_order(tensor_bits)

    def by_partner(operand):
        return jnp.concatenate(
            [
                lax.dynamic_slice_in_dim(operand, (tensor_at ^ place) * own_rows, own_rows, axis=1)
                for place in tensor_order
            ],
            axis=1,
        )

    def in_sequence(operand):
        place_of = jnp.asarray(
            [tensor_order.index(place) for place in range(tensor_count)], jnp.int32
        )
        return jnp.concatenate(
            [
                lax.dynamic_slice_in_dim(
                    operand, place_of[tensor_at ^ place] * own_rows, own_rows, axis=1
                )
                for place in range(tensor_count)
            ],
            axis=1,
        )

    pairs = micro_count * heads_here
    per_device = max(1, pairs // groups)
    copies = max(1, groups // pairs)

    def to_heads(operand, work=None):
        wide = operand.shape[3]
        return pairs_to_heads(
            operand.transpose(0, 2, 1, 3).reshape(pairs, rows_here, wide), work
        )

    def pairs_to_heads(blocks, work=None):
        wide = blocks.shape[2]
        if copies > 1:
            blocks = jnp.repeat(blocks, copies, axis=0)
        arrived = lax.all_to_all(blocks, "expert", split_axis=0, concat_axis=0, tiled=True)
        if work is not None:
            arrived = after(arrived, *work(blocks))
        blocks = arrived.reshape(groups, per_device, rows_here, wide)
        return blocks.transpose(1, 0, 2, 3).reshape(per_device, groups * rows_here, wide)

    def pairs_from_heads(operand, others=()):
        wide = operand.shape[2]
        blocks = operand.reshape(per_device, groups, rows_here, wide).transpose(1, 0, 2, 3)
        blocks = blocks.reshape(groups * per_device, rows_here, wide)
        blocks = lax.all_to_all(blocks, "expert", split_axis=0, concat_axis=0, tiled=True)
        if others:
            blocks = after(blocks, *others)
        if copies > 1:
            blocks = blocks[::copies]
        return blocks

    def from_heads(operand, others=()):
        blocks = pairs_from_heads(operand, others)
        wide = blocks.shape[2]
        return blocks.reshape(micro_count, heads_here, rows_here, wide).transpose(0, 2, 1, 3)

    row_number = jnp.arange(own_rows, dtype=jnp.int32)
    row_in_block = jnp.concatenate(
        [(tensor_at ^ place) * own_rows + row_number for place in tensor_order]
    )
    row_pos = expert_at * rows_here + row_in_block
    frequency = theta_base ** (-(jnp.arange(head_size // 2, dtype=f32) * 2.0 / head_size))
    angles = row_pos.astype(f32)[:, None] * frequency[None, :]
    angles = jnp.concatenate([angles, angles], axis=1)
    cosine = jnp.cos(angles)
    sine = jnp.sin(angles)
    sequence_pos = (
        jnp.arange(groups, dtype=jnp.int32)[:, None] * rows_here + row_in_block[None, :]
    ).reshape(-1)
    causal = sequence_pos[None, :] <= sequence_pos[:, None]

    near, side = 1, tensor_bits[0]
    far = groups // 2
    far_groups = [[2 * place + last for place in range(far)] for last in range(2)]
    copy_count = tensor_count // 2

    def far_exchange(blocks):
        return lax.all_to_all(
            blocks, "expert", split_axis=0, concat_axis=0, axis_index_groups=far_groups, tiled=True
        )

    def gather_far(rows, work=None):
        block = far_exchange(jnp.broadcast_to(rows[None], (far,) + rows.shape))
        if work is not None:
            block = after(block, *work())
        return block.reshape((far * rows.shape[0],) + rows.shape[1:])

    def gather_sides(block, work=None):
        arrived = [swap(block, "expert", near), swap(block, "tensor", side)]
        return after_all(arrived, *work()) if work is not None else arrived

    def gather_diagonal(by_near, by_side):
        half = by_near.shape[0] // 2
        low, high = swap(by_side[:half], "expert", near), swap(by_near[half:], "tensor", side)
        return jnp.concatenate([low, high], axis=0)

    def gather_rest(block, by_near, by_side):
        half = block.shape[0] // 2
        by_both_low = swap(by_side[:half], "expert", near)
        by_both_high = swap(by_near[half:], "tensor", side)
        copies = [[[block, by_near], [by_side, by_both_low, by_both_high]]]
        for bit in tensor_bits[1:]:
            copies = copies + [
                [[swap(piece, "tensor", bit) for piece in call] for call in copy]
                for copy in copies
            ]
        return [[copy[call] for copy in copies] for call in range(2)]

    def add(*terms):
        total = terms[0].astype(f32)
        for term in terms[1:]:
            total = total + term.astype(f32)
        return total

    def reduce_copies(parts, work=None):
        for bit in tensor_bits[1:][::-1]:
            half = len(parts) // 2
            arrived = [swap(part, "tensor", bit) for part in parts[half:]]
            if work is not None and half == 1:
                arrived = after_all(arrived, *work(parts[1]))
            parts = [add(part, other).astype(bf16) for part, other in zip(parts[:half], arrived)]
        return parts[0]

    def reduce_diagonal(second, work=None):
        half, quarter = second.shape[0] // 2, second.shape[0] // 4
        low, high = second[half : half + quarter], second[half + quarter :]
        arrived = [swap(low, "expert", near), swap(high, "tensor", side)]
        return after_all(arrived, *work(low)) if work is not None else arrived

    def side_parts(first, second, from_near, from_side):
        half, quarter = second.shape[0] // 2, second.shape[0] // 4
        near_part = [first[half : half + quarter], add(first[half + quarter :], from_side)]
        side_part = [add(second[:quarter], from_near), second[quarter:half]]
        return [
            jnp.concatenate([part.astype(bf16) for part in parts], axis=0)
            for parts in (near_part, side_part)
        ]

    def reduce_sides(near_part, side_part, work=None):
        arrived = [swap(near_part, "expert", near), swap(side_part, "tensor", side)]
        return after_all(arrived, *work(near_part)) if work is not None else arrived

    def far_block(first, by_near, by_side):
        return add(first[: first.shape[0] // 2], by_near, by_side).astype(bf16)

    def reduce_far(block, work=None):
        parts = far_exchange(block.reshape((far, block.shape[0] // far) + block.shape[1:]))
        if work is not None:
            parts = after(parts, *work(block))
        return parts

    def far_sum(parts):
        return jnp.sum(parts.astype(f32), axis=0)

    high_bits = [bit for bit in expert_bits if bit >= 4]
    low_places = [place for place in range(1, min(4, groups))]

    def columns_of(operand, low_place):
        block = operand.shape[1] // groups
        return jnp.concatenate(
            [
                lax.dynamic_slice_in_dim(
                    operand, (expert_at ^ low_place ^ place) * block, block, axis=1
                )
                for place in partner_order(high_bits)
            ],
            axis=1,
        )

    near_count = min(4, groups)
    near_groups = [
        [first + place for place in range(near_count)] for first in range(0, groups, near_count)
    ]

    def near_exchange(operand):
        block = operand.shape[1] // groups
        high = expert_at - expert_at % near_count
        parts = [
            jnp.concatenate(
                [
                    lax.dynamic_slice_in_dim(
                        operand, ((high ^ above) + place) * block, block, axis=1
                    )
                    for above in partner_order(high_bits)
                ],
                axis=1,
            )
            for place in range(near_count)
        ]
        arrived = lax.all_to_all(
            jnp.stack(parts),
            "expert",
            split_axis=0,
            concat_axis=0,
            axis_index_groups=near_groups,
            tiled=True,
        )
        return arrived.reshape(near_count * flat_rows, -1)

    def near_gather(operand):
        return lax.all_gather(
            operand, "expert", axis_index_groups=near_groups, axis=0, tiled=True
        )

    def near_rows(gathered, place):
        return lax.dynamic_slice_in_dim(
            gathered, ((expert_at % 4) ^ place) * flat_rows, flat_rows, axis=0
        )

    def near_swaps(operand):
        return [swap(operand, "expert", place) for place in low_places]

    def halve_product(product):
        for bit in high_bits[:0:-1]:
            product = halve_rows(product, [("expert", bit)], 0)
        kept_half, sent = jnp.split(product, 2, axis=0)
        return kept_half, swap(sent, "expert", high_bits[0])

    grad_rows = lax.dynamic_slice_in_dim(out_grad, tensor_at * own_rows, own_rows, axis=1)
    route_rows = lax.dynamic_slice_in_dim(routes, tensor_at * own_rows, own_rows, axis=1)
    mask_rows = jnp.sum(
        (route_rows[..., None] == jnp.arange(experts, dtype=jnp.int32)).astype(f32), axis=2
    )
    upstream = jnp.concatenate(
        [grad_rows, jnp.pad(mask_rows, ((0, 0), (0, 0), (0, 128 - experts))).astype(bf16)], axis=2
    )
    upstream = upstream.reshape(micro_count * own_rows, width + 128)
    upstream_gathered = lax.all_gather(upstream, ("expert", "tensor"), axis=0, tiled=True)

    tokens_here = by_partner(tokens)
    flat_tokens = tokens_here.reshape(flat_rows, width)
    norm_in, query_raw, key_raw, value_low, squares = project(
        flat_tokens, norm1_gain, w_query, w_key, w_value
    )
    gains = [query_gain.reshape(1, local_width), key_gain.reshape(1, local_width)]
    head_shape = (micro_count, rows_here, heads_here, head_size)

    def from_partners(operand):
        return [swap(operand, "tensor", place) for place in tensor_order[1:]]

    packed, scales = turn_and_pack(
        query_raw,
        key_raw,
        value_low,
        gains,
        cosine,
        sine,
        squares,
        from_partners(squares),
        own_rows,
        width,
        pairs,
    )
    packed = pairs_to_heads(packed)
    head_parts = []
    for number in range(per_device):
        parts = [
            packed[number, :, part * head_size : (part + 1) * head_size] for part in range(3)
        ]
        head_parts.append((parts, attention_forward(*parts, causal, score_scale)))
    attended = from_heads(jnp.stack([out for _, (out, _) in head_parts]))
    attended = attended.reshape(flat_rows, local_width)

    attn_part = mm(attended, w_output).astype(bf16).reshape(micro_count, rows_here, width)
    halves = jnp.split(attn_part, 2, axis=1)
    attn_half = add(halves[0], swap(halves[1], *tensor_steps[-1]))
    attn_rows = halve_rows(attn_half.astype(bf16), tensor_steps[:-1][::-1], 1, f32)
    own_source = tokens_here[:, :own_rows].astype(f32)
    residual = (own_source + attn_rows).reshape(micro_count * own_rows, width)
    norm_out = (residual * rms_scale(residual) * norm2_gain).astype(bf16)

    expert_base = jnp.reshape(expert_at * owned, (1,)).astype(jnp.int32)
    table = []
    for call in range(2):
        for copy_place in partner_order(tensor_bits[1:]):
            for last in range(2):
                for place in range(far):
                    owner = 2 * place + (expert_at % 2 ^ last)
                    table.append(
                        owner * tensor_count + (tensor_at ^ (copy_place ^ (call * side)))
                    )
    table = jnp.stack(table).astype(jnp.int32)
    upstream_made = []

    def upstream_work(call, token):
        def work():
            upstream_made.append(
                upstream_products(
                    call,
                    2,
                    table,
                    upstream_gathered,
                    w_down,
                    [upstream_made[-1][2]] if upstream_made else [],
                    [token],
                )
            )
            return upstream_made[-1][:1]

        return work

    block = gather_far(norm_out, upstream_work(0, norm_out))
    by_near, by_side = gather_sides(block, upstream_work(1, block))
    gathered = gather_rest(block, by_near, by_side)
    upstream_all = upstream_made[-1][2]
    total_rows = micro_count * groups * rows_here
    kept = []

    def expert_rows(call):
        nonlocal kept
        copies = gathered[call]
        rows = sum(piece.shape[0] for piece in copies[0])
        count = min(copy_count, max(1, expert_rows_most // rows))
        all_parts = []
        for part in range(copy_count // count):
            parts, kept = expert_call(
                call * (copy_count // count) + part,
                total_rows,
                part,
                expert_base,
                copies[part * count : (part + 1) * count],
                rows // 2,
                upstream_made[call][1],
                w_router,
                w_gate,
                w_up,
                upstream_made[call][0],
                kept,
            )
            all_parts += parts
        return all_parts

    made = {}

    def down_work(call):
        def work(token):
            tokens = token if isinstance(token, list) else [token]
            made[call] = down_products(call, 2, copy_count, kept[1], w_down, tokens)
            return list(made[call][:1])

        return work

    def grad_work(name, left, right, *others):
        def work(token):
            tokens = token if isinstance(token, list) else [token]
            made[name] = expert_grads(left, right, owned, tokens)
            return [made[name], *others]

        return work

    attended_gathered = near_gather(attended)
    first = expert_rows(0)
    norm_in_gathered = near_exchange(after(norm_in, first[0]))
    first = reduce_copies(first)
    second = expert_rows(1)
    second = reduce_copies(after_all(second, norm_in_gathered))
    near_part, side_part = side_parts(first, second, *reduce_diagonal(second, lambda token: down_work(0)([token, first])))
    arrived = reduce_sides(
        near_part,
        side_part,
        lambda token: down_work(1)(token) + grad_work("down", kept[1], upstream_all)(token),
    )
    out_first, out_second = (reduce_copies(made[call]) for call in range(2))
    out_diagonal = reduce_diagonal(out_second)
    row_parts = reduce_far(
        far_block(first, *arrived),
        lambda token: [out_first, out_second],
    )
    residual_grad, residual_low, router_part, second_gain_part = rows_back(
        after(row_parts, attended_gathered),
        residual,
        norm_out,
        upstream[:, width:],
        w_router,
        norm2_gain,
        grad_rows.reshape(micro_count * own_rows, width),
    )
    out_sides = reduce_sides(
        *side_parts(out_first, out_second, *after_all(out_diagonal, residual_low))
    )
    residual_grad, residual_low = (
        item.reshape(micro_count, own_rows, width) for item in (residual_grad, residual_low)
    )
    residual_low = jnp.concatenate(
        [residual_low, swap(residual_low, *tensor_steps[0])], axis=1
    )
    residual_low = double_rows(residual_low, tensor_steps[1:], 1).reshape(flat_rows, width)

    attended_grad = mm_t(residual_low, w_output).astype(bf16).reshape(head_shape)
    attended_grad = to_heads(attended_grad, grad_work("up", kept[0], kept[3], *out_sides))
    head_grads = []
    for number in range(per_device):
        parts, (_, log_total) = head_parts[number]
        grads = attention_backward(*parts, log_total, attended_grad[number], causal, score_scale)
        head_grads.append(jnp.concatenate(grads, axis=1))
    residual_gathered = near_exchange(after(residual_low, attended_grad))
    head_grads = after(jnp.stack(head_grads), residual_gathered)
    out_block = far_block(out_first, *after_all(out_sides, attended_grad))
    packed_grad = pairs_from_heads(
        head_grads, grad_work("gate", kept[0], kept[2])(head_grads)
    )
    out_parts = reduce_far(after(out_block, packed_grad))
    normed_q_grad, normed_k_grad, value_grad_low, row_dots, gain_parts = unturn(
        packed_grad, query_raw, key_raw, gains, cosine, sine, scales
    )
    value_arrived = near_swaps(value_grad_low)
    query_grad_low, key_grad_low = norm_back(
        normed_q_grad,
        normed_k_grad,
        query_raw,
        key_raw,
        gains,
        scales,
        row_dots,
        [after(dots, out_parts) for dots in from_partners(row_dots)],
        own_rows,
        width,
    )
    query_arrived = near_swaps(query_grad_low)
    norm_in_there = after(norm_in_gathered, query_grad_low)
    norm_in_near = jnp.concatenate(
        [near_rows(norm_in_there, place) for place in range(near_count)], axis=0
    )

    def near_product(own, arrived, *others):
        right = jnp.concatenate([own] + after_all(arrived, *others), axis=0)
        return t_mm(norm_in_near, right).astype(bf16)

    value_product = near_product(value_grad_low, value_arrived, query_grad_low)
    query_arrived = after_all(query_arrived, value_product)
    key_arrived = near_swaps(after(key_grad_low, *query_arrived))
    query_product = near_product(query_grad_low, query_arrived)
    key_arrived = after_all(key_arrived, query_product)
    key_product = near_product(key_grad_low, key_arrived)
    halves_made = [halve_product(item) for item in (value_product, query_product, key_product)]
    scale_in = rms_scale(tokens_here.astype(f32))
    norm_in_part, first_gain_part = project_back(
        after(query_grad_low, value_product),
        key_grad_low,
        value_grad_low,
        flat_tokens,
        scale_in.reshape(flat_rows, 1),
        w_query,
        w_key,
        w_value,
    )
    halves = jnp.split(norm_in_part.reshape(micro_count, rows_here, width), 2, axis=1)
    norm_in_half = add(halves[0], swap(halves[1], *tensor_steps[-1])).astype(bf16)
    norm_in_grad = halve_rows(norm_in_half, tensor_steps[:-1][::-1], 1, f32)
    output_product = t_mm(residual_gathered, after(attended_gathered, query_grad_low))
    halves_made.append(halve_product(output_product.astype(bf16)))
    own_scale = scale_in[:, :own_rows]
    weighted_in = norm_in_grad * norm1_gain
    tokens_grad = (
        residual_grad
        + own_scale * weighted_in
        - own_source * own_scale**3 * jnp.mean(weighted_in * own_source, axis=2, keepdims=True)
    )
    tokens_low = tokens_grad.astype(bf16)
    tokens_grad = in_sequence(double_rows(tokens_low, tensor_steps, 1)).astype(f32)

    out_rows = far_sum(after(out_parts, tokens_low))
    layer_out = (residual + out_rows).astype(bf16)
    layer_out = layer_out.reshape(micro_count, own_rows, tensor_count, -1).transpose(2, 0, 1, 3)
    layer_out = lax.all_to_all(layer_out, "tensor", split_axis=0, concat_axis=0, tiled=True)
    layer_out = layer_out.transpose(1, 0, 2, 3).reshape(micro_count, rows_here, -1)

    column_block = width // groups

    def reduce_small(rows):
        rows = jnp.pad(rows, ((0, -rows.shape[0] % 16), (0, 0))).astype(bf16)
        rows = rows.reshape(-1, groups, column_block).transpose(1, 0, 2)
        rows = lax.all_to_all(rows, "expert", split_axis=0, concat_axis=0, tiled=True)
        rows = jnp.sum(rows.astype(f32), axis=0).astype(bf16)
        return sum_over(rows, tensor_steps).astype(f32)

    head_block = head_size // groups
    head_gains = gain_parts[:2].reshape(2 * heads_here, groups, head_block)
    head_gains = head_gains.transpose(1, 0, 2).reshape(groups, 2 * heads_here * head_block)
    head_gains = jnp.pad(head_gains, ((0, 0), (0, column_block - head_gains.shape[1])))
    head_rows = jnp.where(
        jnp.arange(tensor_count, dtype=jnp.int32)[:, None] == tensor_at,
        head_gains.reshape(1, width),
        0.0,
    )
    small = reduce_small(
        after(
            jnp.concatenate(
                [router_part, second_gain_part, first_gain_part, head_rows], axis=0
            ),
            tokens_low,
        )
    )
    grad_router = small[:experts].T
    own_heads = lax.dynamic_slice_in_dim(small, experts + 2 + tensor_at, 1, axis=0)
    own_heads = own_heads[0, : 2 * heads_here * head_block].reshape(2, heads_here, head_block)


    grad_value, grad_query, grad_key, grad_output = (
        add(own_half, after(other_half, layer_out)) for own_half, other_half in halves_made
    )
    grad_output = grad_output.T
    return (
        layer_out,
        tokens_grad,
        small[experts + 1],
        grad_query,
        grad_key,
        grad_value,
        own_heads[0],
        own_heads[1],
        grad_output,
        small[experts],
        grad_router,
        made["gate"],
        made["up"],
        made["down"],
    )


def solution(mesh):
    placed = (
        P(None, "expert", None),
        P(None, "expert", None),
        P(None, "expert", None),
        P(),
        P(None, "tensor"),
        P(None, "tensor"),
        P(None, "tensor"),
        P("tensor", None),
        P("tensor", None),
        P("tensor", None),
        P(),
        P(),
        P("expert", None, "tensor"),
        P("expert", None, "tensor"),
        P("expert", "tensor", None),
    )
    return jax.shard_map(
        shards,
        mesh=mesh,
        in_specs=placed,
        out_specs=(
            P(None, "expert", "tensor"),
            P(None, "expert", None),
            P("expert"),
            P("expert", "tensor"),
            P("expert", "tensor"),
            P("expert", "tensor"),
            P("tensor", "expert"),
            P("tensor", "expert"),
            P("tensor", "expert"),
            P("expert"),
            P("expert", None),
            P("expert", None, "tensor"),
            P("expert", None, "tensor"),
            P("expert", "tensor", None),
        ),
        check_vma=False,
    )
```
